512 devices in a mesh: dp: 16 (over x_hi, y, core), mp: 32 (over z, x_lo).
Axes of the slice: x: 4 (x_hi: 2, x_lo: 2; x = x_hi * 2 + x_lo), y: 4, z: 16, core: 2. Of those that a mesh axis runs over, the one named last changes fastest.
Arguments:
- activations: bfloat16 [3072, 8192], P('mp', 'dp'), may hold values from -240 to 240
- w_qkv: bfloat16 [3072, 9216], P(None, 'mp'), may hold values from -0.109375 to 0.109375
- w_out: bfloat16 [3072, 3072], P(None, 'mp'), may hold values from -0.875 to 0.875
- d_branch: bfloat16 [3072, 8192], P('mp', 'dp'), may hold values from -0.25 to 0.25
Outputs:
- branch_out: bfloat16 [3072, 8192], P('mp', 'dp')
- grad_qkv: bfloat16 [3072, 9216], P('dp', 'mp')
- grad_out: bfloat16 [3072, 3072], P('dp', 'mp')
The draws below stay inside these ranges and needn't reach their ends.
All inputs are finite; a program needn't handle non-finite values.
Results may differ from the reference program's by a relative error of at most 0.03.
Values may be sent and summed in bfloat16 or wider, within the bound.
No kernel may reach another device: no remote copies, remote signals or barrier semaphores. Data moves between devices by JAX's collectives and lax.ppermute only.
A program may use at most 64 MiB of HBM per device.

```python
import jax
import jax.numpy as jnp
from jax import lax

D = 3072
HEAD = 96
PATCHES = 256
HEADS = 32
INNER = 3072
TOK_DEV = 512
TOKENS = 8192


def draw_activations(key, part):
    key = jax.random.fold_in(key, 11)
    first_key, second_key = jax.random.split(key, 2)
    position = jnp.arange(D, dtype=jnp.float32) / D
    column_scale = 0.4 * 10.0 ** position
    row_scale = 10.0 ** jax.random.uniform(second_key, (1, TOKENS), jnp.float32, 0.0, 1.0)
    rough = jnp.clip(jax.random.normal(first_key, (D, TOKENS), jnp.float32), -4.0, 4.0)
    result = rough * column_scale[:, None] * row_scale
    return result.astype(jnp.bfloat16)


def raised(values, key, source, target, blocks, factor):
    owner, partner = [(jnp.arange(values.shape[axis_at]) // (values.shape[axis_at] // blocks)).reshape([-1 if axis == axis_at else 1 for axis in range(values.ndim)]) for axis_at in (source, target)]
    chosen = jax.random.permutation(key, blocks)[partner]
    strong = (owner == chosen) | (owner == (partner + blocks // 2) % blocks)
    return jnp.where(strong, factor * values, values)


def level_of(key, extent, shards, low, top_value):
    def one(dim, blocks):
        steps = jax.random.uniform(jax.random.fold_in(jax.random.fold_in(key, 6), dim), (blocks,), jnp.float32, low / len(shards), top_value / len(shards))
        return jnp.repeat(jnp.exp(steps), extent[dim] // blocks).reshape((-1,) + (1,) * (len(extent) - dim - 1))

    level = one(*shards[0])
    for cut in shards[1:]:
        level = level * one(*cut)
    return level


def bell_draw(own_key, dims, deviation, bound, pieces=(), held_as=jnp.bfloat16):
    values = jax.random.normal(own_key, dims, jnp.float32) * deviation
    if len(pieces) > 0:
        values = level_of(own_key, dims, pieces, -0.22, 0.18) * values
    return jnp.clip(values, min=-bound, max=bound).astype(held_as)


def heavy_noise(own_key, extent, spread, reach, shards, heavy, kind=jnp.bfloat16):
    array = spread * jax.random.normal(own_key, extent, jnp.float32)
    if shards:
        array = array * level_of(own_key, extent, shards, -0.22, 0.18)
    return jnp.clip(raised(array, jax.random.fold_in(own_key, 3), *heavy), -reach, reach).astype(kind)


def setup_inputs(seed: int = 0) -> dict:
    key_list = jax.random.split(jax.random.key(seed), 5)
    return {
        "activations": draw_activations(jax.random.fold_in(key_list[4], 71), 0),
        "w_qkv": bell_draw(key_list[1], (D, 3 * INNER), D ** -0.5, 0.109375, ((1, 32),)),
        "w_out": bell_draw(key_list[2], (D, INNER), (INNER // 64) ** -0.5, 0.875, ((1, 32),)),
        "d_branch": heavy_noise(key_list[3], (D, TOKENS), 0.02, 0.25, ((0, 32), (1, 16)), (1, 0, 32, 2.75)),
    }


epsilon = 1e-06
highest = lax.Precision.HIGHEST

def normalize_last(values):
    centre = values - lax.optimization_barrier(jnp.mean(values, -1, keepdims=True))
    inverse = lax.rsqrt(lax.optimization_barrier(jnp.mean(centre * centre, -1, keepdims=True)) + epsilon)
    return (centre * inverse, inverse)

def attend(queries, keys_in, values_in, grad_in):
    query_norm, query_inv = normalize_last(queries.astype(jnp.float32))
    key_norm, key_inv = normalize_last(keys_in.astype(jnp.float32))
    scaling = queries.shape[-1] ** (-0.5)
    scores = jnp.einsum('ipc,iqc->ipq', query_norm, key_norm, precision=highest) * scaling
    exponent = jnp.exp(scores)
    attention = exponent / lax.optimization_barrier(jnp.sum(exponent, -1, keepdims=True))
    attention_low = lax.optimization_barrier(attention.astype(jnp.bfloat16))
    attention_wide = attention_low.astype(jnp.float32)
    values_wide = values_in.astype(jnp.float32)
    grad_wide = grad_in.astype(jnp.float32)
    heads_out = jnp.einsum('ipq,iqc->ipc', attention_wide, values_wide, precision=highest).astype(jnp.bfloat16)
    grad_weights = jnp.einsum('ipc,iqc->ipq', grad_wide, values_wide, precision=highest)
    grad_values = jnp.einsum('ipq,ipc->iqc', attention_wide, grad_wide, precision=highest)
    grad_scores = attention * (grad_weights - lax.optimization_barrier(jnp.sum(grad_weights * attention, -1, keepdims=True)))
    grad_qnorm = jnp.einsum('ipq,iqc->ipc', grad_scores, key_norm, precision=highest) * scaling
    grad_knorm = jnp.einsum('ipq,ipc->iqc', grad_scores, query_norm, precision=highest) * scaling
    grad_query = (grad_qnorm - lax.optimization_barrier(jnp.mean(grad_qnorm, -1, keepdims=True)) - query_norm * lax.optimization_barrier(jnp.mean(grad_qnorm * query_norm, -1, keepdims=True))) * query_inv
    grad_key = (grad_knorm - lax.optimization_barrier(jnp.mean(grad_knorm, -1, keepdims=True)) - key_norm * lax.optimization_barrier(jnp.mean(grad_knorm * key_norm, -1, keepdims=True))) * key_inv
    grad_proj = jnp.concatenate([grad_query, grad_key, grad_values], -1).astype(jnp.bfloat16)
    return (heads_out, grad_proj)

def reference(activations, w_qkv, w_out, d_branch):
    values = activations.astype(jnp.float32)
    centre = values - lax.optimization_barrier(jnp.mean(values, 0))
    normed = (centre * lax.rsqrt(lax.optimization_barrier(jnp.mean(centre * centre, 0)) + epsilon)).astype(jnp.bfloat16)
    projected = jnp.dot(normed.T, w_qkv, preferred_element_type=jnp.float32).astype(jnp.bfloat16)
    grad_heads = jnp.dot(d_branch.T, w_out, preferred_element_type=jnp.float32).astype(jnp.bfloat16)
    images = TOKENS // PATCHES
    per_head = projected.reshape(TOKENS, HEADS, 3 * HEAD).transpose(1, 0, 2)
    grad_per_head = grad_heads.reshape(TOKENS, HEADS, HEAD).transpose(1, 0, 2)
    weight_per_head = w_out.reshape(D, HEADS, HEAD).transpose(1, 0, 2)

    def one_head(total, inputs):
        columns, grad_cols, weight_cols = inputs
        shaped = columns.reshape(images, PATCHES, 3 * HEAD)
        outputs, grad_proj = attend(shaped[..., :HEAD], shaped[..., HEAD:2 * HEAD], shaped[..., 2 * HEAD:], grad_cols.reshape(images, PATCHES, HEAD))
        outputs = outputs.reshape(TOKENS, HEAD)
        term = jnp.dot(weight_cols, outputs.T, preferred_element_type=jnp.float32)
        term = lax.optimization_barrier(term.astype(jnp.bfloat16)).astype(jnp.float32)
        return (total + term, (outputs, grad_proj.reshape(TOKENS, 3 * HEAD)))
    total, stacked = lax.scan(one_head, jnp.zeros((D, TOKENS), jnp.float32), (per_head, grad_per_head, weight_per_head))
    branch_out = total.astype(jnp.bfloat16)
    outputs_cat = stacked[0].transpose(1, 0, 2).reshape(TOKENS, INNER)
    grad_cat = stacked[1].transpose(1, 0, 2).reshape(TOKENS, 3 * INNER)
    blocks = TOKENS // TOK_DEV
    normed_blocks = normed.reshape(D, blocks, TOK_DEV).transpose(1, 0, 2)
    cot_blocks = d_branch.reshape(D, blocks, TOK_DEV).transpose(1, 0, 2)

    def one_block(sums, inputs):
        norm_block, grad_block, cot_block, out_block = inputs
        first = jnp.dot(norm_block, grad_block, preferred_element_type=jnp.float32)
        second = jnp.dot(cot_block, out_block, preferred_element_type=jnp.float32)
        first = lax.optimization_barrier(first.astype(jnp.bfloat16)).astype(jnp.float32)
        second = lax.optimization_barrier(second.astype(jnp.bfloat16)).astype(jnp.float32)
        return ((sums[0] + first, sums[1] + second), None)
    sums, leftover = lax.scan(one_block, (jnp.zeros((D, 3 * INNER), jnp.float32), jnp.zeros((D, INNER), jnp.float32)), (normed_blocks, grad_cat.reshape(blocks, TOK_DEV, 3 * INNER), cot_blocks, outputs_cat.reshape(blocks, TOK_DEV, INNER)))
    return (branch_out, sums[0].astype(jnp.bfloat16), sums[1].astype(jnp.bfloat16))
```

```python
import functools

import jax
import jax.numpy as jnp
from jax import lax
from jax.experimental import pallas as pl
from jax.experimental.pallas import tpu as pltpu
from jax.sharding import Mesh
from jax.sharding import PartitionSpec as P

PATCHES = 256
epsilon = 1e-06
highest = lax.Precision.HIGHEST
low = jnp.bfloat16
wide = jnp.float32


def contract(left, right, left_dim, right_dim, precision=None):
    return lax.dot_general(
        left,
        right,
        (((left_dim,), (right_dim,)), ((), ())),
        precision=precision,
        preferred_element_type=wide,
    )


def normalize_first(values):
    centre = values - jnp.mean(values, 0, keepdims=True)
    inverse = lax.rsqrt(jnp.mean(centre * centre, 0, keepdims=True) + epsilon)
    return (centre * inverse, inverse)


def forward_kernel(
    part, head, gathered, own, other, normed, attention, query, key, inverses, value, heads, branch
):
    features = normed.shape[0]
    blocks = features // part

    def rows_of(block):
        return gathered[pl.ds(pl.multiple_of(2 * part * block, part), part), :].astype(wide)

    zero = jnp.zeros((1, PATCHES), wide)
    total = lax.fori_loop(
        0, blocks, lambda b, t: t + jnp.sum(rows_of(b), 0, keepdims=True), zero
    )
    mean = total / features

    def squares(block, carried):
        centre = rows_of(block) - mean
        return carried + jnp.sum(centre * centre, 0, keepdims=True)

    variance = lax.fori_loop(0, blocks, squares, zero) / features
    scale = lax.rsqrt(variance + epsilon)

    def write(block, carried):
        at = pl.ds(pl.multiple_of(part * block, part), part)
        normed[at, :] = ((rows_of(block) - mean) * scale).astype(low)
        return carried

    lax.fori_loop(0, blocks, write, 0)
    for slot, weights in enumerate((own, other)):
        projected = contract(weights[: 3 * head, :], normed[...], 1, 0).astype(low)
        query_norm, query_inv = normalize_first(projected[:head].astype(wide))
        key_norm, key_inv = normalize_first(projected[head : 2 * head].astype(wide))
        values = projected[2 * head :]
        scores = contract(key_norm, query_norm, 0, 0, highest) * head ** (-0.5)
        exponent = jnp.exp(scores)
        attend = exponent / jnp.sum(exponent, 0, keepdims=True)
        attention[slot] = attend
        query[slot] = query_norm
        key[slot] = key_norm
        inverses[slot, 0:1, :] = query_inv
        inverses[slot, 1:2, :] = key_inv
        value[slot] = values
        heads[slot] = contract(values, attend.astype(low), 1, 0).astype(low)
    both_heads = heads[...].reshape(2 * head, PATCHES)
    step = 512
    for start in range(0, features, step):
        both = jnp.concatenate(
            [own[3 * head :, start : start + step], other[3 * head :, start : start + step]], 0
        )
        branch[start : start + step, :] = contract(both, both_heads, 0, 0).astype(low)


def backward_kernel(
    part,
    head,
    place,
    gathered,
    own,
    other,
    normed,
    attention,
    query,
    key,
    inverses,
    value,
    heads,
    shares,
    cotangent,
):
    features = normed.shape[0]
    blocks = features // part
    for block in range(blocks):
        cotangent[part * block : part * (block + 1), :] = gathered[
            2 * part * block + part : 2 * part * (block + 1), :
        ]
    scaling = head ** (-0.5)
    cores, _, chips, rows, columns = shares.shape
    for slot, weights in enumerate((own, other)):
        grad = contract(weights[...], cotangent[...], 1, 0).astype(low)
        attend = attention[slot]
        query_norm, key_norm = query[slot], key[slot]
        grad_weights = contract(value[slot], grad, 0, 0)
        grad_values = contract(grad, attend.astype(low), 1, 1)
        grad_scores = attend * (grad_weights - jnp.sum(grad_weights * attend, 0, keepdims=True))
        grad_qnorm = contract(key_norm, grad_scores, 1, 0, highest) * scaling
        grad_knorm = contract(query_norm, grad_scores, 1, 1, highest) * scaling
        grad_query = (
            grad_qnorm
            - jnp.mean(grad_qnorm, 0, keepdims=True)
            - query_norm * jnp.mean(grad_qnorm * query_norm, 0, keepdims=True)
        ) * inverses[slot, 0:1, :]
        grad_key = (
            grad_knorm
            - jnp.mean(grad_knorm, 0, keepdims=True)
            - key_norm * jnp.mean(grad_knorm * key_norm, 0, keepdims=True)
        ) * inverses[slot, 1:2, :]
        grad_proj = jnp.concatenate([grad_query, grad_key, grad_values], 0).astype(low)
        tail = jnp.concatenate([grad_proj[256:], jnp.zeros((columns - 3 * head, PATCHES), low)], 0)
        lead = jnp.concatenate([jnp.zeros((3 * head - 256, PATCHES), low), heads[slot]], 0)
        there = place[slot]
        for block in range(cores * chips):
            at = slice(rows * block, rows * (block + 1))
            main = normed[at, :]
            shares[block % cores, there, block // cores, :, :256] = contract(
                main, grad_proj[:256], 1, 1
            ).astype(low)
            shares[block % cores, there, block // cores, :, 256:] = (
                contract(main, tail, 1, 1) + contract(cotangent[at, :], lead, 1, 1)
            ).astype(low)


def on_device(activations, w_qkv, w_out, d_branch):
    part, tokens = activations.shape
    features, head = w_out.shape
    images = tokens // PATCHES
    z, xl, xh, y, core = (lax.axis_size(a) for a in ("z", "xl", "xh", "y", "core"))
    stacked = jnp.stack([activations, d_branch]).reshape(2, part, images, PATCHES)
    mixed = lax.all_to_all(stacked.transpose(2, 0, 1, 3), "xl", 0, 0, tiled=True)
    gathered = lax.all_gather(mixed.reshape(2 * xl * part, PATCHES), "z", axis=0, tiled=True)

    own = jnp.concatenate([w_qkv.T, w_out.T], 0)
    half = own.shape[0] // core
    core_at = lax.axis_index("core")
    swap = [(0, 1), (1, 0)]
    mine = lax.ppermute(lax.dynamic_slice_in_dim(own, core_at * half, half, 0), "xl", swap)
    theirs = lax.ppermute(mine, "core", swap)
    first = core_at == 0
    other = jnp.concatenate([jnp.where(first, mine, theirs), jnp.where(first, theirs, mine)], 0)

    shape = jax.ShapeDtypeStruct
    vmem = pl.BlockSpec(memory_space=pltpu.VMEM)
    kept = (
        shape((features, PATCHES), low),
        shape((2, PATCHES, PATCHES), wide),
        shape((2, head, PATCHES), wide),
        shape((2, head, PATCHES), wide),
        shape((2, 8, PATCHES), wide),
        shape((2, head, PATCHES), low),
        shape((2, head, PATCHES), low),
    )
    *kept, branch = pl.pallas_call(
        functools.partial(forward_kernel, part, head),
        out_shape=kept + (shape((features, PATCHES), low),),
        in_specs=[vmem] * 3,
        out_specs=[vmem] * 8,
        compiler_params=pltpu.CompilerParams(vmem_limit_bytes=40 << 20),
        cost_estimate=pl.CostEstimate(
            flops=2_000_000_000, bytes_accessed=14_000_000, transcendentals=131072
        ),
        name="forward",
    )(gathered, own, other)
    summed = lax.psum_scatter(branch, "z", scatter_dimension=0, tiled=True)

    at = lax.axis_index("xl")
    place = jnp.stack([at, 1 - at]).astype(jnp.int32)
    columns = 4 * head
    rows = features // (core * xh * y)
    shares = pl.pallas_call(
        functools.partial(backward_kernel, part, head),
        out_shape=shape((core, xl, xh * y, rows, columns), low),
        in_specs=[pl.BlockSpec(memory_space=pltpu.SMEM)] + [vmem] * 10,
        out_specs=vmem,
        scratch_shapes=[pltpu.VMEM((features, PATCHES), low)],
        compiler_params=pltpu.CompilerParams(vmem_limit_bytes=40 << 20),
        cost_estimate=pl.CostEstimate(
            flops=2_000_000_000, bytes_accessed=14_000_000, transcendentals=0
        ),
        name="backward",
    )(place, gathered, w_out.T, other[3 * head :], *kept)
    pairs = lax.all_to_all(shares, "core", 0, 0, tiled=True)
    pair_sum = jnp.sum(pairs.astype(wide), 0).astype(low).reshape(xl * xh * y, rows, columns)
    spread = lax.all_to_all(pair_sum, ("xl", "xh", "y"), 0, 0, tiled=True)
    grads = jnp.sum(spread.astype(wide), 0).astype(low)

    swapped = lax.all_to_all(summed.reshape(xl, part, PATCHES), "xl", 0, 0, tiled=True)
    branch_out = swapped.transpose(1, 0, 2).reshape(part, tokens)
    return (branch_out, grads[:, : 3 * head], grads[:, 3 * head :])


def solution(mesh):
    fine = Mesh(mesh.devices.reshape(2, 4, 2, 16, 2), ("xh", "y", "core", "z", "xl"))
    dp, mp = ("xh", "y", "core"), ("z", "xl")
    in_specs = (P(mp, dp), P(None, mp), P(None, mp), P(mp, dp))
    out_specs = (P(mp, dp), P(dp, mp), P(dp, mp))
    return jax.shard_map(
        on_device, mesh=fine, in_specs=in_specs, out_specs=out_specs, check_vma=False
    )
```

```python
import functools

import jax
import jax.numpy as jnp
from jax import lax
from jax.experimental import pallas as pl
from jax.experimental.pallas import tpu as pltpu
from jax.sharding import Mesh
from jax.sharding import PartitionSpec as P

PATCHES = 256
GROUP = 4
epsilon = 1e-06
highest = lax.Precision.HIGHEST
low = jnp.bfloat16
wide = jnp.float32
Z = ("zh", "zl")


def contract(left, right, left_dim, right_dim, precision=None):
    return lax.dot_general(
        left,
        right,
        (((left_dim,), (right_dim,)), ((), ())),
        precision=precision,
        preferred_element_type=wide,
    )


def normalize_first(values):
    centre = values - jnp.mean(values, 0, keepdims=True)
    inverse = lax.rsqrt(jnp.mean(centre * centre, 0, keepdims=True) + epsilon)
    return (centre * inverse, inverse)


def aligned(start, size):
    return pl.ds(pl.multiple_of(start, 16), size)


SETS = ((0, 0, 4), (1, 0, 4), (2, 0, 4), (3, 0, 2), (3, 2, 2))


def forward_kernel(head, place, *refs):
    sets, (qkv_own, out_own, mine, theirs) = refs[:5], refs[5:9]
    normed, attention, query, key, inverses, value, heads = refs[9:16]
    branch_sets = refs[16:21]
    qkv, out, branch, sems = refs[21:]
    features = normed.shape[0]
    block = features // (4 * GROUP)
    core = place[4]
    thirds, quarter = 3 * head // 2, head // 2
    copies = [
        pltpu.make_async_copy(qkv_own, qkv.at[0], sems.at[0]),
        pltpu.make_async_copy(out_own, out.at[0], sems.at[1]),
    ]
    for n, (source, at) in enumerate(((mine, core), (theirs, 1 - core))):
        copies.append(
            pltpu.make_async_copy(
                source.at[pl.ds(0, thirds)], qkv.at[1, aligned(at * thirds, thirds)], sems.at[2 + 2 * n]
            )
        )
        copies.append(
            pltpu.make_async_copy(
                source.at[pl.ds(thirds, quarter)],
                out.at[1, aligned(at * quarter, quarter)],
                sems.at[3 + 2 * n],
            )
        )
    for copy in copies:
        copy.start()

    def over_blocks(body, carried):
        for ref, (which, first, count) in zip(sets, SETS):
            for n in range(count):
                rows = ref[block * n : block * (n + 1), :].astype(wide)
                at = aligned((GROUP * (first + n) + place[which]) * block, block)
                carried = body(rows, at, carried)
        return carried

    def fold(rows):
        return jnp.sum(rows.reshape(block // 8, 8, PATCHES), 0)

    zero = jnp.zeros((8, PATCHES), wide)
    total = over_blocks(lambda rows, at, t: t + fold(rows), zero)
    mean = jnp.sum(total, 0, keepdims=True) / features

    def squares(rows, at, carried):
        centre = rows - mean
        return carried + fold(centre * centre)

    variance = jnp.sum(over_blocks(squares, zero), 0, keepdims=True) / features
    scale = lax.rsqrt(variance + epsilon)

    def write(rows, at, carried):
        normed[at, :] = ((rows - mean) * scale).astype(low)
        return carried

    over_blocks(write, None)
    for copy in copies:
        copy.wait()
    for slot in range(2):
        projected = contract(qkv[slot], normed[...], 1, 0).astype(low)
        query_norm, query_inv = normalize_first(projected[:head].astype(wide))
        key_norm, key_inv = normalize_first(projected[head : 2 * head].astype(wide))
        values = projected[2 * head :]
        scores = contract(key_norm, query_norm, 0, 0, highest) * head ** (-0.5)
        exponent = jnp.exp(scores)
        attend = exponent / jnp.sum(exponent, 0, keepdims=True)
        attention[slot] = attend
        query[slot] = query_norm
        key[slot] = key_norm
        inverses[slot, 0:1, :] = query_inv
        inverses[slot, 1:2, :] = key_inv
        value[slot] = values
        heads[slot] = contract(values, attend.astype(low), 1, 0).astype(low)
    both_heads = heads[...].reshape(2 * head, PATCHES)
    step = 512
    for start in range(0, features, step):
        both = out[:, :, start : start + step].reshape(2 * head, step)
        branch[start : start + step, :] = contract(both, both_heads, 0, 0).astype(low)
    for ref, (which, first, count) in zip(branch_sets, SETS):
        for n in range(count):
            at = aligned((GROUP * (first + n) + place[which]) * block, block)
            ref[block * n : block * (n + 1), :] = branch[at, :]


def backward_kernel(head, place, *refs):
    sets, (out_own, mine, theirs) = refs[:5], refs[5:8]
    normed, attention, query, key, inverses, value, heads = refs[8:15]
    keep, send, cotangent, out, sems = refs[15:]
    core = place[4]
    thirds, quarter = 3 * head // 2, head // 2
    copies = [pltpu.make_async_copy(out_own, out.at[0], sems.at[0])]
    for n, (source, at) in enumerate(((mine, core), (theirs, 1 - core))):
        copies.append(
            pltpu.make_async_copy(
                source.at[pl.ds(thirds, quarter)],
                out.at[1, aligned(at * quarter, quarter)],
                sems.at[1 + n],
            )
        )
    for copy in copies:
        copy.start()
    block = normed.shape[0] // (4 * GROUP)
    for ref, (which, first, count) in zip(sets, SETS):
        for n in range(count):
            at = aligned((GROUP * (first + n) + place[which]) * block, block)
            cotangent[at, :] = ref[block * n : block * (n + 1), :]
    for copy in copies:
        copy.wait()
    scaling = head ** (-0.5)
    _, chips, rows, columns = keep.shape
    for slot in range(2):
        grad = contract(out[slot], cotangent[...], 1, 0).astype(low)
        attend = attention[slot]
        query_norm, key_norm = query[slot], key[slot]
        grad_weights = contract(value[slot], grad, 0, 0)
        grad_values = contract(grad, attend.astype(low), 1, 1)
        grad_scores = attend * (grad_weights - jnp.sum(grad_weights * attend, 0, keepdims=True))
        grad_qnorm = contract(key_norm, grad_scores, 1, 0, highest) * scaling
        grad_knorm = contract(query_norm, grad_scores, 1, 1, highest) * scaling
        grad_query = (
            grad_qnorm
            - jnp.mean(grad_qnorm, 0, keepdims=True)
            - query_norm * jnp.mean(grad_qnorm * query_norm, 0, keepdims=True)
        ) * inverses[slot, 0:1, :]
        grad_key = (
            grad_knorm
            - jnp.mean(grad_knorm, 0, keepdims=True)
            - key_norm * jnp.mean(grad_knorm * key_norm, 0, keepdims=True)
        ) * inverses[slot, 1:2, :]
        grad_proj = jnp.concatenate([grad_query, grad_key, grad_values], 0).astype(low)
        tail = jnp.concatenate([grad_proj[256:], jnp.zeros((columns - 3 * head, PATCHES), low)], 0)
        lead = jnp.concatenate([jnp.zeros((3 * head - 256, PATCHES), low), heads[slot]], 0)
        there = place[5 + slot]
        for ref, owner in ((send, 1 - core), (keep, core)):
            for chip in range(chips):
                at = aligned((2 * chip + owner) * rows, rows)
                main = normed[at, :]
                ref[there, chip, :, :256] = contract(main, grad_proj[:256], 1, 1).astype(low)
                ref[there, chip, :, 256:] = (
                    contract(main, tail, 1, 1) + contract(cotangent[at, :], lead, 1, 1)
                ).astype(low)


def shift(values, by):
    size = lax.axis_size(Z)
    return lax.ppermute(values, Z, [(i, (i + by) % size) for i in range(size)])


def on_device(activations, w_qkv, w_out, d_branch):
    part, tokens = activations.shape
    features, head = w_out.shape
    images = tokens // PATCHES
    zh, xl, xh, y, core = (lax.axis_size(a) for a in ("zh", "xl", "xh", "y", "core"))
    swap = [(0, 1), (1, 0)]
    core_at, xl_at, residue = (lax.axis_index(a) for a in ("core", "xl", "zl"))
    place = jnp.stack(
        [
            residue,
            (residue + 1) % GROUP,
            (residue + 3) % GROUP,
            (residue + 2) % GROUP,
            core_at,
            xl_at,
            1 - xl_at,
        ]
    ).astype(jnp.int32)

    def by_image(values):
        return values.reshape(part, images, PATCHES).transpose(1, 0, 2)

    qkv_own, out_own = w_qkv.T, w_out.T
    thirds, quarter = 3 * head // 2, head // 2
    mine = jnp.concatenate(
        [
            lax.dynamic_slice_in_dim(qkv_own, core_at * thirds, thirds, 0),
            lax.dynamic_slice_in_dim(out_own, core_at * quarter, quarter, 0),
        ],
        0,
    )
    mine = lax.ppermute(mine, "xl", swap)

    def same_residue(values):
        copies = jnp.broadcast_to(by_image(values)[None], (zh, images, part, PATCHES))
        return lax.all_to_all(
            copies.reshape(zh * images, part, PATCHES), ("zh", "xl"), 0, 0, tiled=True
        ).reshape(zh * xl * part, PATCHES)

    def other_residues(same):
        middle = same.shape[0] // 2
        return (
            same,
            shift(same, -1),
            shift(same, 1),
            shift(same[:middle], 2),
            shift(same[middle:], -2),
        )

    same = same_residue(activations)
    mine, d_branch, same = lax.optimization_barrier((mine, d_branch, same))
    sets = other_residues(same)
    theirs = lax.ppermute(mine, "core", swap)
    cotangent_sets = other_residues(same_residue(d_branch))

    shape = jax.ShapeDtypeStruct
    vmem = pl.BlockSpec(memory_space=pltpu.VMEM)
    smem = pl.BlockSpec(memory_space=pltpu.SMEM)
    anywhere = pl.BlockSpec(memory_space=pl.ANY)
    kept = (
        shape((features, PATCHES), low),
        shape((2, PATCHES, PATCHES), wide),
        shape((2, head, PATCHES), wide),
        shape((2, head, PATCHES), wide),
        shape((2, 8, PATCHES), wide),
        shape((2, head, PATCHES), low),
        shape((2, head, PATCHES), low),
    )
    outputs = pl.pallas_call(
        functools.partial(forward_kernel, head),
        out_shape=kept + tuple(shape(s.shape, low) for s in sets),
        in_specs=[smem] + [vmem] * 5 + [anywhere] * 4,
        out_specs=[vmem] * 12,
        scratch_shapes=[
            pltpu.VMEM((2, 3 * head, features), low),
            pltpu.VMEM((2, head, features), low),
            pltpu.VMEM((features, PATCHES), low),
            pltpu.SemaphoreType.DMA((6,)),
        ],
        compiler_params=pltpu.CompilerParams(vmem_limit_bytes=40 << 20),
        cost_estimate=pl.CostEstimate(
            flops=2_000_000_000, bytes_accessed=14_000_000, transcendentals=131072
        ),
        name="forward",
    )(place, *sets, qkv_own, out_own, mine, theirs)
    kept, (b_own, b_plus, b_minus, b_lead, b_tail) = outputs[:7], outputs[7:]
    halves = jnp.concatenate([shift(b_lead, 2), shift(b_tail, -2)], 0)
    terms = (b_own, shift(b_plus, 1), shift(b_minus, -1), halves)
    summed = sum(t.astype(wide) for t in terms).astype(low)
    spread = lax.all_to_all(
        summed.reshape(zh * xl, part, PATCHES), ("zh", "xl"), 0, 0, tiled=True
    ).reshape(zh, xl, part, PATCHES)
    branch_out = jnp.sum(spread.astype(wide), 0).astype(low).transpose(1, 0, 2).reshape(part, tokens)

    columns = 4 * head
    rows = features // (core * xh * y)
    share = shape((xl, xh * y, rows, columns), low)
    keep, send = pl.pallas_call(
        functools.partial(backward_kernel, head),
        out_shape=(share, share),
        in_specs=[smem] + [vmem] * 5 + [anywhere] * 3 + [vmem] * 7,
        out_specs=(vmem, vmem),
        scratch_shapes=[
            pltpu.VMEM((features, PATCHES), low),
            pltpu.VMEM((2, head, features), low),
            pltpu.SemaphoreType.DMA((3,)),
        ],
        compiler_params=pltpu.CompilerParams(vmem_limit_bytes=40 << 20),
        cost_estimate=pl.CostEstimate(
            flops=2_000_000_000, bytes_accessed=14_000_000, transcendentals=0
        ),
        name="backward",
    )(place, *cotangent_sets, out_own, mine, theirs, *kept)
    received = lax.ppermute(send, "core", swap)
    pair_sum = (keep.astype(wide) + received.astype(wide)).astype(low)
    grads = lax.all_to_all(
        pair_sum.reshape(xl * xh * y, rows, columns), ("xl", "xh", "y"), 0, 0, tiled=True
    )
    grads = jnp.sum(grads.astype(wide), 0).astype(low)
    return (branch_out, grads[:, : 3 * head], grads[:, 3 * head :])


def solution(mesh):
    fine = Mesh(mesh.devices.reshape(2, 4, 2, 4, 4, 2), ("xh", "y", "core", "zh", "zl", "xl"))
    dp, mp = ("xh", "y", "core"), ("zh", "zl", "xl")
    in_specs = (P(mp, dp), P(None, mp), P(None, mp), P(mp, dp))
    out_specs = (P(mp, dp), P(dp, mp), P(dp, mp))
    return jax.shard_map(
        on_device, mesh=fine, in_specs=in_specs, out_specs=out_specs, check_vma=False
    )
```

```python
import functools

import jax
import jax.numpy as jnp
from jax import lax
from jax.experimental import pallas as pl
from jax.experimental.pallas import tpu as pltpu
from jax.sharding import Mesh
from jax.sharding import PartitionSpec as P

PATCHES = 256
GROUP = 4
epsilon = 1e-06
highest = lax.Precision.HIGHEST
low = jnp.bfloat16
wide = jnp.float32
Z = ("zh", "zl")


def contract(left, right, left_dim, right_dim, precision=None):
    return lax.dot_general(
        left,
        right,
        (((left_dim,), (right_dim,)), ((), ())),
        precision=precision,
        preferred_element_type=wide,
    )


def normalize_first(values):
    centre = values - jnp.mean(values, 0, keepdims=True)
    inverse = lax.rsqrt(jnp.mean(centre * centre, 0, keepdims=True) + epsilon)
    return (centre * inverse, inverse)


def aligned(start, size):
    return pl.ds(pl.multiple_of(start, 16), size)


SETS = ((0, 0, 4), (1, 0, 4), (2, 0, 4), (3, 0, 2), (3, 2, 2))


def forward_kernel(head, place, *refs):
    sets, (qkv_own, out_own, mine, theirs) = refs[:5], refs[5:9]
    normed, attention, query, key, inverses, value, heads = refs[9:16]
    branch, qkv, out, sems = refs[16:]
    features = normed.shape[0]
    block = features // (4 * GROUP)
    core = place[4]
    thirds, quarter = 3 * head // 2, head // 2
    copies = [
        pltpu.make_async_copy(qkv_own, qkv.at[0], sems.at[0]),
        pltpu.make_async_copy(out_own, out.at[0], sems.at[1]),
    ]
    for n, (source, at) in enumerate(((mine, core), (theirs, 1 - core))):
        copies.append(
            pltpu.make_async_copy(
                source.at[pl.ds(0, thirds)], qkv.at[1, aligned(at * thirds, thirds)], sems.at[2 + 2 * n]
            )
        )
        copies.append(
            pltpu.make_async_copy(
                source.at[pl.ds(thirds, quarter)],
                out.at[1, aligned(at * quarter, quarter)],
                sems.at[3 + 2 * n],
            )
        )
    for copy in copies:
        copy.start()

    def over_blocks(body, carried):
        for ref, (which, first, count) in zip(sets, SETS):
            for n in range(count):
                rows = ref[block * n : block * (n + 1), :].astype(wide)
                at = aligned((GROUP * (first + n) + place[which]) * block, block)
                carried = body(rows, at, carried)
        return carried

    def fold(rows):
        return jnp.sum(rows.reshape(block // 8, 8, PATCHES), 0)

    zero = jnp.zeros((8, PATCHES), wide)
    total = over_blocks(lambda rows, at, t: t + fold(rows), zero)
    mean = jnp.sum(total, 0, keepdims=True) / features

    def squares(rows, at, carried):
        centre = rows - mean
        return carried + fold(centre * centre)

    variance = jnp.sum(over_blocks(squares, zero), 0, keepdims=True) / features
    scale = lax.rsqrt(variance + epsilon)

    def write(rows, at, carried):
        normed[at, :] = ((rows - mean) * scale).astype(low)
        return carried

    over_blocks(write, None)
    for copy in copies:
        copy.wait()
    for slot in range(2):
        projected = contract(qkv[slot], normed[...], 1, 0).astype(low)
        query_norm, query_inv = normalize_first(projected[:head].astype(wide))
        key_norm, key_inv = normalize_first(projected[head : 2 * head].astype(wide))
        values = projected[2 * head :]
        scores = contract(key_norm, query_norm, 0, 0, highest) * head ** (-0.5)
        exponent = jnp.exp(scores)
        attend = exponent / jnp.sum(exponent, 0, keepdims=True)
        attention[slot] = attend
        query[slot] = query_norm
        key[slot] = key_norm
        inverses[slot, 0:1, :] = query_inv
        inverses[slot, 1:2, :] = key_inv
        value[slot] = values
        heads[slot] = contract(values, attend.astype(low), 1, 0).astype(low)
    both_heads = heads[...].reshape(2 * head, PATCHES)
    step = 512
    for start in range(0, features, step):
        both = out[:, :, start : start + step].reshape(2 * head, step)
        branch[start : start + step, :] = contract(both, both_heads, 0, 0).astype(low)


def backward_kernel(head, place, cotangent, out_own, mine, theirs, *refs):
    normed, attention, query, key, inverses, value, heads = refs[:7]
    shares, out, sems = refs[7:]
    core = place[4]
    thirds, quarter = 3 * head // 2, head // 2
    copies = [pltpu.make_async_copy(out_own, out.at[0], sems.at[0])]
    for n, (source, at) in enumerate(((mine, core), (theirs, 1 - core))):
        copies.append(
            pltpu.make_async_copy(
                source.at[pl.ds(thirds, quarter)],
                out.at[1, aligned(at * quarter, quarter)],
                sems.at[1 + n],
            )
        )
    for copy in copies:
        copy.start()
    for copy in copies:
        copy.wait()
    scaling = head ** (-0.5)
    cores, _, chips, rows, columns = shares.shape
    for slot in range(2):
        grad = contract(out[slot], cotangent[...], 1, 0).astype(low)
        attend = attention[slot]
        query_norm, key_norm = query[slot], key[slot]
        grad_weights = contract(value[slot], grad, 0, 0)
        grad_values = contract(grad, attend.astype(low), 1, 1)
        grad_scores = attend * (grad_weights - jnp.sum(grad_weights * attend, 0, keepdims=True))
        grad_qnorm = contract(key_norm, grad_scores, 1, 0, highest) * scaling
        grad_knorm = contract(query_norm, grad_scores, 1, 1, highest) * scaling
        grad_query = (
            grad_qnorm
            - jnp.mean(grad_qnorm, 0, keepdims=True)
            - query_norm * jnp.mean(grad_qnorm * query_norm, 0, keepdims=True)
        ) * inverses[slot, 0:1, :]
        grad_key = (
            grad_knorm
            - jnp.mean(grad_knorm, 0, keepdims=True)
            - key_norm * jnp.mean(grad_knorm * key_norm, 0, keepdims=True)
        ) * inverses[slot, 1:2, :]
        grad_proj = jnp.concatenate([grad_query, grad_key, grad_values], 0).astype(low)
        tail = jnp.concatenate([grad_proj[256:], jnp.zeros((columns - 3 * head, PATCHES), low)], 0)
        lead = jnp.concatenate([jnp.zeros((3 * head - 256, PATCHES), low), heads[slot]], 0)
        there = place[5 + slot]
        for owner in range(cores):
            for chip in range(chips):
                at = slice((2 * chip + owner) * rows, (2 * chip + owner + 1) * rows)
                main = normed[at, :]
                shares[owner, there, chip, :, :256] = contract(main, grad_proj[:256], 1, 1).astype(low)
                shares[owner, there, chip, :, 256:] = (
                    contract(main, tail, 1, 1) + contract(cotangent[at, :], lead, 1, 1)
                ).astype(low)


def shift(values, by):
    size = lax.axis_size(Z)
    return lax.ppermute(values, Z, [(i, (i + by) % size) for i in range(size)])


def on_device(activations, w_qkv, w_out, d_branch):
    part, tokens = activations.shape
    features, head = w_out.shape
    images = tokens // PATCHES
    zh, xl, xh, y, core = (lax.axis_size(a) for a in ("zh", "xl", "xh", "y", "core"))
    swap = [(0, 1), (1, 0)]
    core_at, xl_at, residue = (lax.axis_index(a) for a in ("core", "xl", "zl"))
    place = jnp.stack(
        [
            residue,
            (residue + 1) % GROUP,
            (residue + 3) % GROUP,
            (residue + 2) % GROUP,
            core_at,
            xl_at,
            1 - xl_at,
        ]
    ).astype(jnp.int32)

    def by_image(values):
        return values.reshape(part, images, PATCHES).transpose(1, 0, 2)

    mixed = lax.all_to_all(by_image(d_branch), "xl", 0, 0, tiled=True)

    qkv_own, out_own = w_qkv.T, w_out.T
    thirds, quarter = 3 * head // 2, head // 2
    mine = jnp.concatenate(
        [
            lax.dynamic_slice_in_dim(qkv_own, core_at * thirds, thirds, 0),
            lax.dynamic_slice_in_dim(out_own, core_at * quarter, quarter, 0),
        ],
        0,
    )
    mine, activations, mixed = lax.optimization_barrier((mine, activations, mixed))
    cotangent = lax.all_gather(mixed.reshape(xl * part, PATCHES), Z, axis=0, tiled=True)
    mine = lax.ppermute(mine, "xl", swap)
    copies = jnp.broadcast_to(by_image(activations)[None], (zh, images, part, PATCHES))
    same = lax.all_to_all(
        copies.reshape(zh * images, part, PATCHES), ("zh", "xl"), 0, 0, tiled=True
    ).reshape(zh * xl * part, PATCHES)
    mine, same = lax.optimization_barrier((mine, same))
    theirs = lax.ppermute(mine, "core", swap)
    middle = zh * xl * part // 2
    sets = (
        same,
        shift(same, -1),
        shift(same, 1),
        shift(same[:middle], 2),
        shift(same[middle:], -2),
    )

    shape = jax.ShapeDtypeStruct
    vmem = pl.BlockSpec(memory_space=pltpu.VMEM)
    smem = pl.BlockSpec(memory_space=pltpu.SMEM)
    anywhere = pl.BlockSpec(memory_space=pl.ANY)
    kept = (
        shape((features, PATCHES), low),
        shape((2, PATCHES, PATCHES), wide),
        shape((2, head, PATCHES), wide),
        shape((2, head, PATCHES), wide),
        shape((2, 8, PATCHES), wide),
        shape((2, head, PATCHES), low),
        shape((2, head, PATCHES), low),
    )
    outputs = pl.pallas_call(
        functools.partial(forward_kernel, head),
        out_shape=kept + (shape((features, PATCHES), low),),
        in_specs=[smem] + [vmem] * 5 + [anywhere] * 4,
        out_specs=[vmem] * 8,
        scratch_shapes=[
            pltpu.VMEM((2, 3 * head, features), low),
            pltpu.VMEM((2, head, features), low),
            pltpu.SemaphoreType.DMA((6,)),
        ],
        compiler_params=pltpu.CompilerParams(vmem_limit_bytes=40 << 20),
        cost_estimate=pl.CostEstimate(
            flops=2_000_000_000, bytes_accessed=14_000_000, transcendentals=131072
        ),
        name="forward",
    )(place, *sets, qkv_own, out_own, mine, theirs)
    kept, branch = outputs[:7], outputs[7]
    summed = lax.psum_scatter(branch, Z, scatter_dimension=0, tiled=True)
    columns = 4 * head
    rows = features // (core * xh * y)
    shares = pl.pallas_call(
        functools.partial(backward_kernel, head),
        out_shape=shape((core, xl, xh * y, rows, columns), low),
        in_specs=[smem, vmem] + [anywhere] * 3 + [vmem] * 7,
        out_specs=vmem,
        scratch_shapes=[pltpu.VMEM((2, head, features), low), pltpu.SemaphoreType.DMA((3,))],
        compiler_params=pltpu.CompilerParams(vmem_limit_bytes=40 << 20),
        cost_estimate=pl.CostEstimate(
            flops=1_000_000, bytes_accessed=100_000, transcendentals=0
        ),
        name="backward",
    )(place, cotangent, out_own, mine, theirs, *kept)
    pairs = lax.all_to_all(shares, "core", 0, 0, tiled=True)
    pair_sum = jnp.sum(pairs.astype(wide), 0).astype(low)
    grads = lax.all_to_all(
        pair_sum.reshape(xl * xh * y, rows, columns), ("xl", "xh", "y"), 0, 0, tiled=True
    )
    summed, grads = lax.optimization_barrier((summed, grads))
    grads = jnp.sum(grads.astype(wide), 0).astype(low)
    swapped = lax.all_to_all(summed.reshape(xl, part, PATCHES), "xl", 0, 0, tiled=True)
    branch_out = swapped.transpose(1, 0, 2).reshape(part, tokens)
    return (branch_out, grads[:, : 3 * head], grads[:, 3 * head :])


def solution(mesh):
    fine = Mesh(mesh.devices.reshape(2, 4, 2, 4, 4, 2), ("xh", "y", "core", "zh", "zl", "xl"))
    dp, mp = ("xh", "y", "core"), ("zh", "zl", "xl")
    in_specs = (P(mp, dp), P(None, mp), P(None, mp), P(mp, dp))
    out_specs = (P(mp, dp), P(dp, mp), P(dp, mp))
    return jax.shard_map(
        on_device, mesh=fine, in_specs=in_specs, out_specs=out_specs, check_vma=False
    )
```

```python
import functools

import jax
import jax.numpy as jnp
from jax import lax
from jax.experimental import pallas as pl
from jax.experimental.pallas import tpu as pltpu
from jax.sharding import Mesh
from jax.sharding import PartitionSpec as P

PATCHES = 256
GROUP = 4
epsilon = 1e-06
highest = lax.Precision.HIGHEST
low = jnp.bfloat16
wide = jnp.float32
Z = ("zh", "zl")


def contract(left, right, left_dim, right_dim, precision=None):
    return lax.dot_general(
        left,
        right,
        (((left_dim,), (right_dim,)), ((), ())),
        precision=precision,
        preferred_element_type=wide,
    )


def normalize_first(values):
    centre = values - jnp.mean(values, 0, keepdims=True)
    inverse = lax.rsqrt(jnp.mean(centre * centre, 0, keepdims=True) + epsilon)
    return (centre * inverse, inverse)


def aligned(start, size):
    return pl.ds(pl.multiple_of(start, 16), size)


SETS = ((0, 0, 4), (1, 0, 4), (2, 0, 4), (3, 0, 2), (3, 2, 2))


def start_all(pairs, sems, first=0):
    copies = [
        pltpu.make_async_copy(source, target, sems.at[first + n])
        for n, (source, target) in enumerate(pairs)
    ]
    for copy in copies:
        copy.start()
    return copies


def wait_all(copies):
    for copy in copies:
        copy.wait()


def partner_pieces(mine, theirs, core, first, size):
    for source, at in ((mine, core), (theirs, 1 - core)):
        yield source.at[pl.ds(first, size)], aligned(at * size, size)


def forward_kernel(head, place, *refs):
    gathered, qkv_own, out_own, mine, theirs = refs[:5]
    results, branch_result = refs[5:12], refs[12]
    raw, qkv, out, branch = refs[13:17]
    kept, sems = refs[17:24], refs[24]
    normed, attention, query, key, inverses, value, heads = kept
    features = normed.shape[0]
    block = features // (4 * GROUP)
    core = place[4]
    thirds, quarter = 3 * head // 2, head // 2
    rows_in = start_all([(gathered, raw)], sems)
    weights_in = [(qkv_own, qkv.at[0]), (out_own, out.at[0])]
    for source, at in partner_pieces(mine, theirs, core, 0, thirds):
        weights_in.append((source, qkv.at[1, at]))
    for source, at in partner_pieces(mine, theirs, core, thirds, quarter):
        weights_in.append((source, out.at[1, at]))
    weights_in = start_all(weights_in, sems, 1)
    wait_all(rows_in)

    def rows_of(n):
        return raw[block * n : block * (n + 1), :].astype(wide)

    def fold(rows):
        return jnp.sum(rows.reshape(block // 8, 8, PATCHES), 0)

    blocks = range(4 * GROUP)
    mean = jnp.sum(sum(fold(rows_of(n)) for n in blocks), 0, keepdims=True) / features
    variance = sum(fold((rows_of(n) - mean) * (rows_of(n) - mean)) for n in blocks)
    scale = lax.rsqrt(jnp.sum(variance, 0, keepdims=True) / features + epsilon)
    for n in blocks:
        normed[block * n : block * (n + 1), :] = ((rows_of(n) - mean) * scale).astype(low)
    results_out = start_all([(normed, results[0])], sems, 7)
    wait_all(weights_in)
    for slot in range(2):
        projected = contract(qkv[slot], normed[...], 1, 0).astype(low)
        query_norm, query_inv = normalize_first(projected[:head].astype(wide))
        key_norm, key_inv = normalize_first(projected[head : 2 * head].astype(wide))
        values = projected[2 * head :]
        scores = contract(key_norm, query_norm, 0, 0, highest) * head ** (-0.5)
        exponent = jnp.exp(scores)
        attend = exponent / jnp.sum(exponent, 0, keepdims=True)
        attention[slot] = attend
        query[slot] = query_norm
        key[slot] = key_norm
        inverses[slot, 0:1, :] = query_inv
        inverses[slot, 1:2, :] = key_inv
        value[slot] = values
        heads[slot] = contract(values, attend.astype(low), 1, 0).astype(low)
    results_out += start_all(list(zip(kept[1:], results[1:])), sems, 8)
    both_heads = heads[...].reshape(2 * head, PATCHES)
    step = 768
    for n, start in enumerate(range(0, features, step)):
        both = out[:, :, start : start + step].reshape(2 * head, step)
        branch[start : start + step, :] = contract(both, both_heads, 0, 0).astype(low)
        part = pl.ds(start, step)
        results_out += start_all([(branch.at[part], branch_result.at[part])], sems, 14 + n)
    wait_all(results_out)


def backward_kernel(head, place, *refs):
    results, sets, (out_own, mine, theirs) = refs[:7], refs[7:12], refs[12:15]
    shares, cotangent, out = refs[15:18]
    kept, sems = refs[18:25], refs[25]
    normed, attention, query, key, inverses, value, heads = kept
    core = place[4]
    thirds, quarter = 3 * head // 2, head // 2
    block = cotangent.shape[0] // (4 * GROUP)
    first_in = [(out_own, out.at[0])]
    for ref, (which, first, count) in zip(sets, SETS):
        for n in range(count):
            at = aligned((GROUP * (first + n) + place[which]) * block, block)
            first_in.append((ref.at[pl.ds(block * n, block)], cotangent.at[at]))
    for source, at in partner_pieces(mine, theirs, core, thirds, quarter):
        first_in.append((source, out.at[1, at]))
    first_in = start_all(first_in, sems)
    kept_in = start_all(list(zip(results[1:], kept[1:])) + [(results[0], normed)], sems, 19)
    wait_all(first_in)
    scaling = head ** (-0.5)
    cores, _, chips, rows, columns = shares.shape
    grads = [contract(out[slot], cotangent[...], 1, 0).astype(low) for slot in range(2)]
    wait_all(kept_in[:-1])
    rights = []
    for slot, grad in enumerate(grads):
        attend = attention[slot]
        query_norm, key_norm = query[slot], key[slot]
        grad_weights = contract(value[slot], grad, 0, 0)
        grad_values = contract(grad, attend.astype(low), 1, 1)
        grad_scores = attend * (grad_weights - jnp.sum(grad_weights * attend, 0, keepdims=True))
        grad_qnorm = contract(key_norm, grad_scores, 1, 0, highest) * scaling
        grad_knorm = contract(query_norm, grad_scores, 1, 1, highest) * scaling
        grad_query = (
            grad_qnorm
            - jnp.mean(grad_qnorm, 0, keepdims=True)
            - query_norm * jnp.mean(grad_qnorm * query_norm, 0, keepdims=True)
        ) * inverses[slot, 0:1, :]
        grad_key = (
            grad_knorm
            - jnp.mean(grad_knorm, 0, keepdims=True)
            - key_norm * jnp.mean(grad_knorm * key_norm, 0, keepdims=True)
        ) * inverses[slot, 1:2, :]
        grad_proj = jnp.concatenate([grad_query, grad_key, grad_values], 0).astype(low)
        tail = jnp.concatenate([grad_proj[256:], jnp.zeros((columns - 3 * head, PATCHES), low)], 0)
        lead = jnp.concatenate([jnp.zeros((3 * head - 256, PATCHES), low), heads[slot]], 0)
        rights.append((grad_proj[:256], tail, lead))
    wait_all(kept_in[-1:])
    for slot, (main_right, tail, lead) in enumerate(rights):
        there = place[5 + slot]
        for owner in range(cores):
            for chip in range(chips):
                at = slice((2 * chip + owner) * rows, (2 * chip + owner + 1) * rows)
                main = normed[at, :]
                shares[owner, there, chip, :, :256] = contract(main, main_right, 1, 1).astype(low)
                shares[owner, there, chip, :, 256:] = (
                    contract(main, tail, 1, 1) + contract(cotangent[at, :], lead, 1, 1)
                ).astype(low)


def shift(values, by):
    size = lax.axis_size(Z)
    return lax.ppermute(values, Z, [(i, (i + by) % size) for i in range(size)])


def on_device(activations, w_qkv, w_out, d_branch):
    part, tokens = activations.shape
    features, head = w_out.shape
    images = tokens // PATCHES
    zh, xl, xh, y, core = (lax.axis_size(a) for a in ("zh", "xl", "xh", "y", "core"))
    swap = [(0, 1), (1, 0)]
    core_at, xl_at, residue = (lax.axis_index(a) for a in ("core", "xl", "zl"))
    place = jnp.stack(
        [
            residue,
            (residue + 1) % GROUP,
            (residue + 3) % GROUP,
            (residue + 2) % GROUP,
            core_at,
            xl_at,
            1 - xl_at,
        ]
    ).astype(jnp.int32)

    def by_image(values):
        return values.reshape(part, images, PATCHES).transpose(1, 0, 2)

    mixed = lax.all_to_all(by_image(activations), "xl", 0, 0, tiled=True)

    qkv_own, out_own = w_qkv.T, w_out.T
    thirds, quarter = 3 * head // 2, head // 2
    mine = jnp.concatenate(
        [
            lax.dynamic_slice_in_dim(qkv_own, core_at * thirds, thirds, 0),
            lax.dynamic_slice_in_dim(out_own, core_at * quarter, quarter, 0),
        ],
        0,
    )
    mine, d_branch, mixed = lax.optimization_barrier((mine, d_branch, mixed))
    gathered = lax.all_gather(mixed.reshape(xl * part, PATCHES), Z, axis=0, tiled=True)
    mine = lax.ppermute(mine, "xl", swap)
    copies = jnp.broadcast_to(by_image(d_branch)[None], (zh, images, part, PATCHES))
    same = lax.all_to_all(
        copies.reshape(zh * images, part, PATCHES), ("zh", "xl"), 0, 0, tiled=True
    ).reshape(zh * xl * part, PATCHES)
    middle = zh * xl * part // 2
    mine, same = lax.optimization_barrier((mine, same))
    theirs = lax.ppermute(mine, "core", swap)
    sets = (
        same,
        shift(same, -1),
        shift(same, 1),
        shift(same[:middle], 2),
        shift(same[middle:], -2),
    )
    gathered, _ = lax.optimization_barrier((gathered, same))

    shape = jax.ShapeDtypeStruct
    vmem = pl.BlockSpec(memory_space=pltpu.VMEM)
    smem = pl.BlockSpec(memory_space=pltpu.SMEM)
    hbm = pl.BlockSpec(memory_space=pltpu.HBM)
    kept = (
        shape((features, PATCHES), low),
        shape((2, PATCHES, PATCHES), wide),
        shape((2, head, PATCHES), wide),
        shape((2, head, PATCHES), wide),
        shape((2, 8, PATCHES), wide),
        shape((2, head, PATCHES), low),
        shape((2, head, PATCHES), low),
    )
    outputs = pl.pallas_call(
        functools.partial(forward_kernel, head),
        out_shape=kept + (shape((features, PATCHES), low),),
        in_specs=[smem] + [hbm] * 5,
        out_specs=[hbm] * 8,
        scratch_shapes=[
            pltpu.VMEM((features, PATCHES), low),
            pltpu.VMEM((2, 3 * head, features), low),
            pltpu.VMEM((2, head, features), low),
            pltpu.VMEM((features, PATCHES), low),
        ]
        + [pltpu.VMEM(k.shape, k.dtype) for k in kept]
        + [pltpu.SemaphoreType.DMA((18,))],
        compiler_params=pltpu.CompilerParams(vmem_limit_bytes=40 << 20),
        cost_estimate=pl.CostEstimate(
            flops=2_000_000_000, bytes_accessed=14_000_000, transcendentals=131072
        ),
        name="forward",
    )(place, gathered, qkv_own, out_own, mine, theirs)
    kept, branch = outputs[:7], outputs[7]
    summed = lax.psum_scatter(branch, Z, scatter_dimension=0, tiled=True)
    columns = 4 * head
    rows = features // (core * xh * y)
    shares = pl.pallas_call(
        functools.partial(backward_kernel, head),
        out_shape=shape((core, xl, xh * y, rows, columns), low),
        in_specs=[smem] + [hbm] * 15,
        out_specs=vmem,
        scratch_shapes=[
            pltpu.VMEM((features, PATCHES), low),
            pltpu.VMEM((2, head, features), low),
        ]
        + [pltpu.VMEM(k.shape, k.dtype) for k in kept]
        + [pltpu.SemaphoreType.DMA((26,))],
        compiler_params=pltpu.CompilerParams(vmem_limit_bytes=40 << 20),
        cost_estimate=pl.CostEstimate(
            flops=1_000_000, bytes_accessed=100_000, transcendentals=0
        ),
        name="backward",
    )(place, *kept, *sets, out_own, mine, theirs)
    pairs = lax.all_to_all(shares, "core", 0, 0, tiled=True)
    pair_sum = jnp.sum(pairs.astype(wide), 0).astype(low)
    grads = lax.all_to_all(
        pair_sum.reshape(xl * xh * y, rows, columns), ("xl", "xh", "y"), 0, 0, tiled=True
    )
    summed, grads = lax.optimization_barrier((summed, grads))
    grads = jnp.sum(grads.astype(wide), 0).astype(low)
    swapped = lax.all_to_all(summed.reshape(xl, part, PATCHES), "xl", 0, 0, tiled=True)
    branch_out = swapped.transpose(1, 0, 2).reshape(part, tokens)
    return (branch_out, grads[:, : 3 * head], grads[:, 3 * head :])


def solution(mesh):
    fine = Mesh(mesh.devices.reshape(2, 4, 2, 4, 4, 2), ("xh", "y", "core", "zh", "zl", "xl"))
    dp, mp = ("xh", "y", "core"), ("zh", "zl", "xl")
    in_specs = (P(mp, dp), P(None, mp), P(None, mp), P(mp, dp))
    out_specs = (P(mp, dp), P(dp, mp), P(dp, mp))
    return jax.shard_map(
        on_device, mesh=fine, in_specs=in_specs, out_specs=out_specs, check_vma=False
    )
```

```python
import functools

import jax
import jax.numpy as jnp
from jax import lax
from jax.experimental import pallas as pl
from jax.experimental.pallas import tpu as pltpu
from jax.sharding import Mesh
from jax.sharding import PartitionSpec as P

PATCHES = 256
GROUP = 4
epsilon = 1e-06
highest = lax.Precision.HIGHEST
low = jnp.bfloat16
wide = jnp.float32
Z = ("zh", "zl")


def contract(left, right, left_dim, right_dim, precision=None):
    return lax.dot_general(
        left,
        right,
        (((left_dim,), (right_dim,)), ((), ())),
        precision=precision,
        preferred_element_type=wide,
    )


def normalize_first(values):
    centre = values - jnp.mean(values, 0, keepdims=True)
    inverse = lax.rsqrt(jnp.mean(centre * centre, 0, keepdims=True) + epsilon)
    return (centre * inverse, inverse)


def aligned(start, size):
    return pl.ds(pl.multiple_of(start, 16), size)


SETS = ((0, 0, 4), (1, 0, 4), (2, 0, 4), (3, 0, 2), (3, 2, 2))


def start_all(pairs, sems, first=0):
    copies = [
        pltpu.make_async_copy(source, target, sems.at[first + n])
        for n, (source, target) in enumerate(pairs)
    ]
    for copy in copies:
        copy.start()
    return copies


def wait_all(copies):
    for copy in copies:
        copy.wait()


def partner_pieces(mine, theirs, core, first, size):
    for source, at in ((mine, core), (theirs, 1 - core)):
        yield source.at[pl.ds(first, size)], aligned(at * size, size)


def forward_kernel(head, place, *refs):
    sets, (qkv_own, out_own, mine, theirs) = refs[:5], refs[5:9]
    results, branch_result = refs[9:16], refs[16]
    raw, qkv, out, branch = refs[17:21]
    kept, sems = refs[21:28], refs[28]
    normed, attention, query, key, inverses, value, heads = kept
    features = normed.shape[0]
    block = features // (4 * GROUP)
    core = place[4]
    thirds, quarter = 3 * head // 2, head // 2
    rows_in = []
    for ref, (which, first, count) in zip(sets, SETS):
        for n in range(count):
            at = aligned((GROUP * (first + n) + place[which]) * block, block)
            rows_in.append((ref.at[pl.ds(block * n, block)], raw.at[at]))
    rows_in = start_all(rows_in, sems)
    weights_in = [(qkv_own, qkv.at[0]), (out_own, out.at[0])]
    for source, at in partner_pieces(mine, theirs, core, 0, thirds):
        weights_in.append((source, qkv.at[1, at]))
    for source, at in partner_pieces(mine, theirs, core, thirds, quarter):
        weights_in.append((source, out.at[1, at]))
    weights_in = start_all(weights_in, sems, 16)
    wait_all(rows_in)

    def rows_of(n):
        return raw[block * n : block * (n + 1), :].astype(wide)

    def fold(rows):
        return jnp.sum(rows.reshape(block // 8, 8, PATCHES), 0)

    blocks = range(4 * GROUP)
    mean = jnp.sum(sum(fold(rows_of(n)) for n in blocks), 0, keepdims=True) / features
    variance = sum(fold((rows_of(n) - mean) * (rows_of(n) - mean)) for n in blocks)
    scale = lax.rsqrt(jnp.sum(variance, 0, keepdims=True) / features + epsilon)
    for n in blocks:
        normed[block * n : block * (n + 1), :] = ((rows_of(n) - mean) * scale).astype(low)
    results_out = start_all([(normed, results[0])], sems, 22)
    wait_all(weights_in)
    for slot in range(2):
        projected = contract(qkv[slot], normed[...], 1, 0).astype(low)
        query_norm, query_inv = normalize_first(projected[:head].astype(wide))
        key_norm, key_inv = normalize_first(projected[head : 2 * head].astype(wide))
        values = projected[2 * head :]
        scores = contract(key_norm, query_norm, 0, 0, highest) * head ** (-0.5)
        exponent = jnp.exp(scores)
        attend = exponent / jnp.sum(exponent, 0, keepdims=True)
        attention[slot] = attend
        query[slot] = query_norm
        key[slot] = key_norm
        inverses[slot, 0:1, :] = query_inv
        inverses[slot, 1:2, :] = key_inv
        value[slot] = values
        heads[slot] = contract(values, attend.astype(low), 1, 0).astype(low)
    results_out += start_all(list(zip(kept[1:], results[1:])), sems, 23)
    both_heads = heads[...].reshape(2 * head, PATCHES)
    step = 768
    for n, start in enumerate(range(0, features, step)):
        both = out[:, :, start : start + step].reshape(2 * head, step)
        branch[start : start + step, :] = contract(both, both_heads, 0, 0).astype(low)
        part = pl.ds(start, step)
        results_out += start_all([(branch.at[part], branch_result.at[part])], sems, 29 + n)
    wait_all(results_out)


def backward_kernel(head, place, *refs):
    results, cotangent_in, out_own, mine, theirs = refs[:7], refs[7], refs[8], refs[9], refs[10]
    shares, cotangent, out = refs[11:14]
    kept, sems = refs[14:21], refs[21]
    normed, attention, query, key, inverses, value, heads = kept
    core = place[4]
    thirds, quarter = 3 * head // 2, head // 2
    first_in = [(cotangent_in, cotangent), (out_own, out.at[0])]
    for source, at in partner_pieces(mine, theirs, core, thirds, quarter):
        first_in.append((source, out.at[1, at]))
    first_in = start_all(first_in, sems)
    kept_in = start_all(list(zip(results[1:], kept[1:])) + [(results[0], normed)], sems, 4)
    wait_all(first_in)
    scaling = head ** (-0.5)
    cores, _, chips, rows, columns = shares.shape
    grads = [contract(out[slot], cotangent[...], 1, 0).astype(low) for slot in range(2)]
    wait_all(kept_in[:-1])
    rights = []
    for slot, grad in enumerate(grads):
        attend = attention[slot]
        query_norm, key_norm = query[slot], key[slot]
        grad_weights = contract(value[slot], grad, 0, 0)
        grad_values = contract(grad, attend.astype(low), 1, 1)
        grad_scores = attend * (grad_weights - jnp.sum(grad_weights * attend, 0, keepdims=True))
        grad_qnorm = contract(key_norm, grad_scores, 1, 0, highest) * scaling
        grad_knorm = contract(query_norm, grad_scores, 1, 1, highest) * scaling
        grad_query = (
            grad_qnorm
            - jnp.mean(grad_qnorm, 0, keepdims=True)
            - query_norm * jnp.mean(grad_qnorm * query_norm, 0, keepdims=True)
        ) * inverses[slot, 0:1, :]
        grad_key = (
            grad_knorm
            - jnp.mean(grad_knorm, 0, keepdims=True)
            - key_norm * jnp.mean(grad_knorm * key_norm, 0, keepdims=True)
        ) * inverses[slot, 1:2, :]
        grad_proj = jnp.concatenate([grad_query, grad_key, grad_values], 0).astype(low)
        tail = jnp.concatenate([grad_proj[256:], jnp.zeros((columns - 3 * head, PATCHES), low)], 0)
        lead = jnp.concatenate([jnp.zeros((3 * head - 256, PATCHES), low), heads[slot]], 0)
        rights.append((grad_proj[:256], tail, lead))
    wait_all(kept_in[-1:])
    for slot, (main_right, tail, lead) in enumerate(rights):
        there = place[5 + slot]
        for owner in range(cores):
            for chip in range(chips):
                at = slice((2 * chip + owner) * rows, (2 * chip + owner + 1) * rows)
                main = normed[at, :]
                shares[owner, there, chip, :, :256] = contract(main, main_right, 1, 1).astype(low)
                shares[owner, there, chip, :, 256:] = (
                    contract(main, tail, 1, 1) + contract(cotangent[at, :], lead, 1, 1)
                ).astype(low)


def shift(values, by):
    size = lax.axis_size(Z)
    return lax.ppermute(values, Z, [(i, (i + by) % size) for i in range(size)])


def on_device(activations, w_qkv, w_out, d_branch):
    part, tokens = activations.shape
    features, head = w_out.shape
    images = tokens // PATCHES
    zh, xl, xh, y, core = (lax.axis_size(a) for a in ("zh", "xl", "xh", "y", "core"))
    swap = [(0, 1), (1, 0)]
    core_at, xl_at, residue = (lax.axis_index(a) for a in ("core", "xl", "zl"))
    place = jnp.stack(
        [
            residue,
            (residue + 1) % GROUP,
            (residue + 3) % GROUP,
            (residue + 2) % GROUP,
            core_at,
            xl_at,
            1 - xl_at,
        ]
    ).astype(jnp.int32)

    stacked = jnp.stack([activations, d_branch]).reshape(2, part, images, PATCHES)
    mixed = lax.all_to_all(stacked.transpose(2, 0, 1, 3), "xl", 0, 0, tiled=True)

    qkv_own, out_own = w_qkv.T, w_out.T
    thirds, quarter = 3 * head // 2, head // 2
    mine = jnp.concatenate(
        [
            lax.dynamic_slice_in_dim(qkv_own, core_at * thirds, thirds, 0),
            lax.dynamic_slice_in_dim(out_own, core_at * quarter, quarter, 0),
        ],
        0,
    )
    mine, mixed = lax.optimization_barrier((mine, mixed))
    chunk = xl * part
    cotangent = lax.all_gather(mixed[:, 1].reshape(chunk, PATCHES), Z, axis=0, tiled=True)
    mine = lax.ppermute(mine, "xl", swap)
    copies = jnp.broadcast_to(mixed[:, 0].reshape(1, chunk, PATCHES), (zh, chunk, PATCHES))
    same = lax.all_to_all(copies, "zh", 0, 0, tiled=True).reshape(zh * chunk, PATCHES)
    mine, same = lax.optimization_barrier((mine, same))
    theirs = lax.ppermute(mine, "core", swap)
    middle = zh * chunk // 2
    sets = (
        same,
        shift(same, -1),
        shift(same, 1),
        shift(same[:middle], 2),
        shift(same[middle:], -2),
    )

    shape = jax.ShapeDtypeStruct
    vmem = pl.BlockSpec(memory_space=pltpu.VMEM)
    smem = pl.BlockSpec(memory_space=pltpu.SMEM)
    hbm = pl.BlockSpec(memory_space=pltpu.HBM)
    kept = (
        shape((features, PATCHES), low),
        shape((2, PATCHES, PATCHES), wide),
        shape((2, head, PATCHES), wide),
        shape((2, head, PATCHES), wide),
        shape((2, 8, PATCHES), wide),
        shape((2, head, PATCHES), low),
        shape((2, head, PATCHES), low),
    )
    outputs = pl.pallas_call(
        functools.partial(forward_kernel, head),
        out_shape=kept + (shape((features, PATCHES), low),),
        in_specs=[smem] + [hbm] * 9,
        out_specs=[hbm] * 8,
        scratch_shapes=[
            pltpu.VMEM((features, PATCHES), low),
            pltpu.VMEM((2, 3 * head, features), low),
            pltpu.VMEM((2, head, features), low),
            pltpu.VMEM((features, PATCHES), low),
        ]
        + [pltpu.VMEM(k.shape, k.dtype) for k in kept]
        + [pltpu.SemaphoreType.DMA((33,))],
        compiler_params=pltpu.CompilerParams(vmem_limit_bytes=60 << 20),
        cost_estimate=pl.CostEstimate(
            flops=2_000_000_000, bytes_accessed=14_000_000, transcendentals=131072
        ),
        name="forward",
    )(place, *sets, qkv_own, out_own, mine, theirs)
    kept, branch = outputs[:7], outputs[7]
    summed = lax.psum_scatter(branch, Z, scatter_dimension=0, tiled=True)
    columns = 4 * head
    rows = features // (core * xh * y)
    shares = pl.pallas_call(
        functools.partial(backward_kernel, head),
        out_shape=shape((core, xl, xh * y, rows, columns), low),
        in_specs=[smem] + [hbm] * 11,
        out_specs=vmem,
        scratch_shapes=[
            pltpu.VMEM((features, PATCHES), low),
            pltpu.VMEM((2, head, features), low),
        ]
        + [pltpu.VMEM(k.shape, k.dtype) for k in kept]
        + [pltpu.SemaphoreType.DMA((11,))],
        compiler_params=pltpu.CompilerParams(vmem_limit_bytes=60 << 20),
        cost_estimate=pl.CostEstimate(
            flops=1_000_000, bytes_accessed=100_000, transcendentals=0
        ),
        name="backward",
    )(place, *kept, cotangent, out_own, mine, theirs)
    pairs = lax.all_to_all(shares, "core", 0, 0, tiled=True)
    pair_sum = jnp.sum(pairs.astype(wide), 0).astype(low)
    grads = lax.all_to_all(
        pair_sum.reshape(xl * xh * y, rows, columns), ("xl", "xh", "y"), 0, 0, tiled=True
    )
    summed, grads = lax.optimization_barrier((summed, grads))
    grads = jnp.sum(grads.astype(wide), 0).astype(low)
    swapped = lax.all_to_all(summed.reshape(xl, part, PATCHES), "xl", 0, 0, tiled=True)
    branch_out = swapped.transpose(1, 0, 2).reshape(part, tokens)
    return (branch_out, grads[:, : 3 * head], grads[:, 3 * head :])


def solution(mesh):
    fine = Mesh(mesh.devices.reshape(2, 4, 2, 4, 4, 2), ("xh", "y", "core", "zh", "zl", "xl"))
    dp, mp = ("xh", "y", "core"), ("zh", "zl", "xl")
    in_specs = (P(mp, dp), P(None, mp), P(None, mp), P(mp, dp))
    out_specs = (P(mp, dp), P(dp, mp), P(dp, mp))
    return jax.shard_map(
        on_device, mesh=fine, in_specs=in_specs, out_specs=out_specs, check_vma=False
    )
```

```python
import functools

import jax
import jax.numpy as jnp
from jax import lax
from jax.experimental import pallas as pl
from jax.experimental.pallas import tpu as pltpu
from jax.sharding import Mesh
from jax.sharding import PartitionSpec as P

PATCHES = 256
GROUP = 4
epsilon = 1e-06
highest = lax.Precision.HIGHEST
low = jnp.bfloat16
wide = jnp.float32
Z = ("zh", "zl")


def contract(left, right, left_dim, right_dim, precision=None):
    return lax.dot_general(
        left,
        right,
        (((left_dim,), (right_dim,)), ((), ())),
        precision=precision,
        preferred_element_type=wide,
    )


def normalize_first(values):
    centre = values - jnp.mean(values, 0, keepdims=True)
    inverse = lax.rsqrt(jnp.mean(centre * centre, 0, keepdims=True) + epsilon)
    return (centre * inverse, inverse)


def aligned(start, size):
    return pl.ds(pl.multiple_of(start, 16), size)


SETS = ((0, 0, 4), (1, 0, 4), (2, 0, 4), (3, 0, 2), (3, 2, 2))


def start_all(pairs, sems, first=0):
    copies = [
        pltpu.make_async_copy(source, target, sems.at[first + n])
        for n, (source, target) in enumerate(pairs)
    ]
    for copy in copies:
        copy.start()
    return copies


def wait_all(copies):
    for copy in copies:
        copy.wait()


def partner_pieces(mine, theirs, core, first, size):
    for source, at in ((mine, core), (theirs, 1 - core)):
        yield source.at[pl.ds(first, size)], aligned(at * size, size)


def rows_from(sets, place, target, part, which_array):
    for ref, (which, first, count) in zip(sets, SETS):
        for n in range(2 * count):
            at = ((GROUP * (first + n // 2) + place[which]) * 2 + n % 2) * part
            yield ref.at[pl.ds((2 * n + which_array) * part, part)], target.at[aligned(at, part)]


def forward_kernel(part, head, place, *refs):
    sets, (qkv_own, out_own, mine, theirs) = refs[:5], refs[5:9]
    results, branch_result = refs[9:16], refs[16]
    raw, qkv, out, branch = refs[17:21]
    kept, sems = refs[21:28], refs[28]
    normed, attention, query, key, inverses, value, heads = kept
    features = normed.shape[0]
    block = features // (4 * GROUP)
    core = place[4]
    thirds, quarter = 3 * head // 2, head // 2
    rows_in = start_all(rows_from(sets, place, raw, part, 0), sems)
    weights_in = [(qkv_own, qkv.at[0]), (out_own, out.at[0])]
    for source, at in partner_pieces(mine, theirs, core, 0, thirds):
        weights_in.append((source, qkv.at[1, at]))
    for source, at in partner_pieces(mine, theirs, core, thirds, quarter):
        weights_in.append((source, out.at[1, at]))
    weights_in = start_all(weights_in, sems, 32)
    wait_all(rows_in)

    def rows_of(n):
        return raw[block * n : block * (n + 1), :].astype(wide)

    def fold(rows):
        return jnp.sum(rows.reshape(block // 8, 8, PATCHES), 0)

    blocks = range(4 * GROUP)
    mean = jnp.sum(sum(fold(rows_of(n)) for n in blocks), 0, keepdims=True) / features
    variance = sum(fold((rows_of(n) - mean) * (rows_of(n) - mean)) for n in blocks)
    scale = lax.rsqrt(jnp.sum(variance, 0, keepdims=True) / features + epsilon)
    for n in blocks:
        normed[block * n : block * (n + 1), :] = ((rows_of(n) - mean) * scale).astype(low)
    results_out = start_all([(normed, results[0])], sems, 38)
    wait_all(weights_in)
    for slot in range(2):
        projected = contract(qkv[slot], normed[...], 1, 0).astype(low)
        query_norm, query_inv = normalize_first(projected[:head].astype(wide))
        key_norm, key_inv = normalize_first(projected[head : 2 * head].astype(wide))
        values = projected[2 * head :]
        scores = contract(key_norm, query_norm, 0, 0, highest) * head ** (-0.5)
        exponent = jnp.exp(scores)
        attend = exponent / jnp.sum(exponent, 0, keepdims=True)
        attention[slot] = attend
        query[slot] = query_norm
        key[slot] = key_norm
        inverses[slot, 0:1, :] = query_inv
        inverses[slot, 1:2, :] = key_inv
        value[slot] = values
        heads[slot] = contract(values, attend.astype(low), 1, 0).astype(low)
    results_out += start_all(list(zip(kept[1:], results[1:])), sems, 39)
    both_heads = heads[...].reshape(2 * head, PATCHES)
    step = 768
    for n, start in enumerate(range(0, features, step)):
        both = out[:, :, start : start + step].reshape(2 * head, step)
        branch[start : start + step, :] = contract(both, both_heads, 0, 0).astype(low)
        part = pl.ds(start, step)
        results_out += start_all([(branch.at[part], branch_result.at[part])], sems, 45 + n)
    wait_all(results_out)


def backward_kernel(part, head, place, *refs):
    results, sets, (out_own, mine, theirs) = refs[:7], refs[7:12], refs[12:15]
    shares, cotangent, out = refs[15:18]
    kept, sems = refs[18:25], refs[25]
    normed, attention, query, key, inverses, value, heads = kept
    core = place[4]
    thirds, quarter = 3 * head // 2, head // 2
    first_in = [(out_own, out.at[0])]
    for source, at in partner_pieces(mine, theirs, core, thirds, quarter):
        first_in.append((source, out.at[1, at]))
    first_in = start_all([*rows_from(sets, place, cotangent, part, 1), *first_in], sems)
    kept_in = start_all(list(zip(results[1:], kept[1:])) + [(results[0], normed)], sems, 35)
    wait_all(first_in)
    scaling = head ** (-0.5)
    cores, _, chips, rows, columns = shares.shape
    grads = [contract(out[slot], cotangent[...], 1, 0).astype(low) for slot in range(2)]
    wait_all(kept_in[:-1])
    rights = []
    for slot, grad in enumerate(grads):
        attend = attention[slot]
        query_norm, key_norm = query[slot], key[slot]
        grad_weights = contract(value[slot], grad, 0, 0)
        grad_values = contract(grad, attend.astype(low), 1, 1)
        grad_scores = attend * (grad_weights - jnp.sum(grad_weights * attend, 0, keepdims=True))
        grad_qnorm = contract(key_norm, grad_scores, 1, 0, highest) * scaling
        grad_knorm = contract(query_norm, grad_scores, 1, 1, highest) * scaling
        grad_query = (
            grad_qnorm
            - jnp.mean(grad_qnorm, 0, keepdims=True)
            - query_norm * jnp.mean(grad_qnorm * query_norm, 0, keepdims=True)
        ) * inverses[slot, 0:1, :]
        grad_key = (
            grad_knorm
            - jnp.mean(grad_knorm, 0, keepdims=True)
            - key_norm * jnp.mean(grad_knorm * key_norm, 0, keepdims=True)
        ) * inverses[slot, 1:2, :]
        grad_proj = jnp.concatenate([grad_query, grad_key, grad_values], 0).astype(low)
        tail = jnp.concatenate([grad_proj[256:], jnp.zeros((columns - 3 * head, PATCHES), low)], 0)
        lead = jnp.concatenate([jnp.zeros((3 * head - 256, PATCHES), low), heads[slot]], 0)
        rights.append((grad_proj[:256], tail, lead))
    wait_all(kept_in[-1:])
    for slot, (main_right, tail, lead) in enumerate(rights):
        there = place[5 + slot]
        for owner in range(cores):
            for chip in range(chips):
                at = slice((2 * chip + owner) * rows, (2 * chip + owner + 1) * rows)
                main = normed[at, :]
                shares[owner, there, chip, :, :256] = contract(main, main_right, 1, 1).astype(low)
                shares[owner, there, chip, :, 256:] = (
                    contract(main, tail, 1, 1) + contract(cotangent[at, :], lead, 1, 1)
                ).astype(low)


def shift(values, by):
    size = lax.axis_size(Z)
    return lax.ppermute(values, Z, [(i, (i + by) % size) for i in range(size)])


def on_device(activations, w_qkv, w_out, d_branch):
    part, tokens = activations.shape
    features, head = w_out.shape
    images = tokens // PATCHES
    zh, xl, xh, y, core = (lax.axis_size(a) for a in ("zh", "xl", "xh", "y", "core"))
    swap = [(0, 1), (1, 0)]
    core_at, xl_at, residue = (lax.axis_index(a) for a in ("core", "xl", "zl"))
    place = jnp.stack(
        [
            residue,
            (residue + 1) % GROUP,
            (residue + 3) % GROUP,
            (residue + 2) % GROUP,
            core_at,
            xl_at,
            1 - xl_at,
        ]
    ).astype(jnp.int32)

    stacked = jnp.stack([activations, d_branch]).reshape(2, part, images, PATCHES)
    mixed = lax.all_to_all(stacked.transpose(2, 0, 1, 3), "xl", 0, 0, tiled=True)

    qkv_own, out_own = w_qkv.T, w_out.T
    thirds, quarter = 3 * head // 2, head // 2
    mine = jnp.concatenate(
        [
            lax.dynamic_slice_in_dim(qkv_own, core_at * thirds, thirds, 0),
            lax.dynamic_slice_in_dim(out_own, core_at * quarter, quarter, 0),
        ],
        0,
    )
    mine, mixed = lax.optimization_barrier((mine, mixed))
    mine = lax.ppermute(mine, "xl", swap)
    same = lax.all_gather(mixed.reshape(xl * 2 * part, PATCHES), "zh", axis=0, tiled=True)
    mine, same = lax.optimization_barrier((mine, same))
    theirs = lax.ppermute(mine, "core", swap)
    middle = same.shape[0] // 2
    sets = (
        same,
        shift(same, -1),
        shift(same, 1),
        shift(same[:middle], 2),
        shift(same[middle:], -2),
    )

    shape = jax.ShapeDtypeStruct
    vmem = pl.BlockSpec(memory_space=pltpu.VMEM)
    smem = pl.BlockSpec(memory_space=pltpu.SMEM)
    hbm = pl.BlockSpec(memory_space=pltpu.HBM)
    kept = (
        shape((features, PATCHES), low),
        shape((2, PATCHES, PATCHES), wide),
        shape((2, head, PATCHES), wide),
        shape((2, head, PATCHES), wide),
        shape((2, 8, PATCHES), wide),
        shape((2, head, PATCHES), low),
        shape((2, head, PATCHES), low),
    )
    outputs = pl.pallas_call(
        functools.partial(forward_kernel, part, head),
        out_shape=kept + (shape((features, PATCHES), low),),
        in_specs=[smem] + [hbm] * 9,
        out_specs=[hbm] * 8,
        scratch_shapes=[
            pltpu.VMEM((features, PATCHES), low),
            pltpu.VMEM((2, 3 * head, features), low),
            pltpu.VMEM((2, head, features), low),
            pltpu.VMEM((features, PATCHES), low),
        ]
        + [pltpu.VMEM(k.shape, k.dtype) for k in kept]
        + [pltpu.SemaphoreType.DMA((49,))],
        compiler_params=pltpu.CompilerParams(vmem_limit_bytes=60 << 20),
        cost_estimate=pl.CostEstimate(
            flops=2_000_000_000, bytes_accessed=14_000_000, transcendentals=131072
        ),
        name="forward",
    )(place, *sets, qkv_own, out_own, mine, theirs)
    kept, branch = outputs[:7], outputs[7]
    summed = lax.psum_scatter(branch, Z, scatter_dimension=0, tiled=True)
    columns = 4 * head
    rows = features // (core * xh * y)
    shares = pl.pallas_call(
        functools.partial(backward_kernel, part, head),
        out_shape=shape((core, xl, xh * y, rows, columns), low),
        in_specs=[smem] + [hbm] * 15,
        out_specs=vmem,
        scratch_shapes=[
            pltpu.VMEM((features, PATCHES), low),
            pltpu.VMEM((2, head, features), low),
        ]
        + [pltpu.VMEM(k.shape, k.dtype) for k in kept]
        + [pltpu.SemaphoreType.DMA((42,))],
        compiler_params=pltpu.CompilerParams(vmem_limit_bytes=60 << 20),
        cost_estimate=pl.CostEstimate(
            flops=1_000_000, bytes_accessed=100_000, transcendentals=0
        ),
        name="backward",
    )(place, *kept, *sets, out_own, mine, theirs)
    pairs = lax.all_to_all(shares, "core", 0, 0, tiled=True)
    pair_sum = jnp.sum(pairs.astype(wide), 0).astype(low)
    grads = lax.all_to_all(
        pair_sum.reshape(xl * xh * y, rows, columns), ("xl", "xh", "y"), 0, 0, tiled=True
    )
    summed, grads = lax.optimization_barrier((summed, grads))
    grads = jnp.sum(grads.astype(wide), 0).astype(low)
    swapped = lax.all_to_all(summed.reshape(xl, part, PATCHES), "xl", 0, 0, tiled=True)
    branch_out = swapped.transpose(1, 0, 2).reshape(part, tokens)
    return (branch_out, grads[:, : 3 * head], grads[:, 3 * head :])


def solution(mesh):
    fine = Mesh(mesh.devices.reshape(2, 4, 2, 4, 4, 2), ("xh", "y", "core", "zh", "zl", "xl"))
    dp, mp = ("xh", "y", "core"), ("zh", "zl", "xl")
    in_specs = (P(mp, dp), P(None, mp), P(None, mp), P(mp, dp))
    out_specs = (P(mp, dp), P(dp, mp), P(dp, mp))
    return jax.shard_map(
        on_device, mesh=fine, in_specs=in_specs, out_specs=out_specs, check_vma=False
    )
```

```python
import functools

import jax
import jax.numpy as jnp
from jax import lax
from jax.experimental import pallas as pl
from jax.experimental.pallas import tpu as pltpu
from jax.sharding import Mesh
from jax.sharding import PartitionSpec as P

PATCHES = 256
epsilon = 1e-06
highest = lax.Precision.HIGHEST
low = jnp.bfloat16
wide = jnp.float32
Z = ("zh", "zl")


def contract(left, right, left_dim, right_dim, precision=None):
    return lax.dot_general(
        left,
        right,
        (((left_dim,), (right_dim,)), ((), ())),
        precision=precision,
        preferred_element_type=wide,
    )


def normalize_first(values):
    centre = values - jnp.mean(values, 0, keepdims=True)
    inverse = lax.rsqrt(jnp.mean(centre * centre, 0, keepdims=True) + epsilon)
    return (centre * inverse, inverse)


def aligned(start, size):
    return pl.ds(pl.multiple_of(start, 16), size)


def start_all(pairs, sems, first=0):
    copies = [
        pltpu.make_async_copy(source, target, sems.at[first + n])
        for n, (source, target) in enumerate(pairs)
    ]
    for copy in copies:
        copy.start()
    return copies


def wait_all(copies):
    for copy in copies:
        copy.wait()


def partner_pieces(mine, theirs, core, first, size):
    for source, at in ((mine, core), (theirs, 1 - core)):
        yield source.at[pl.ds(first, size)], aligned(at * size, size)


def forward_kernel(head, place, *refs):
    gathered, qkv_own, out_own, mine, theirs = refs[:5]
    results, branch_result = refs[5:12], refs[12]
    raw, qkv, out, branch = refs[13:17]
    kept, sems = refs[17:24], refs[24]
    normed, attention, query, key, inverses, value, heads = kept
    features = normed.shape[0]
    core = place[0]
    thirds, quarter = 3 * head // 2, head // 2
    rows_in = start_all([(gathered.at[:, 0], raw)], sems)
    weights_in = [(qkv_own, qkv.at[0]), (out_own, out.at[0])]
    for source, at in partner_pieces(mine, theirs, core, 0, thirds):
        weights_in.append((source, qkv.at[1, at]))
    for source, at in partner_pieces(mine, theirs, core, thirds, quarter):
        weights_in.append((source, out.at[1, at]))
    weights_in = start_all(weights_in, sems, 1)
    wait_all(rows_in)

    blocks, part, _ = raw.shape

    def rows_of(n):
        return raw[n].astype(wide)

    def fold(rows):
        return jnp.sum(rows.reshape(part // 8, 8, PATCHES), 0)

    blocks = range(blocks)
    mean = jnp.sum(sum(fold(rows_of(n)) for n in blocks), 0, keepdims=True) / features
    variance = sum(fold((rows_of(n) - mean) * (rows_of(n) - mean)) for n in blocks)
    scale = lax.rsqrt(jnp.sum(variance, 0, keepdims=True) / features + epsilon)
    for n in blocks:
        normed[part * n : part * (n + 1), :] = ((rows_of(n) - mean) * scale).astype(low)
    results_out = start_all([(normed, results[0])], sems, 7)
    wait_all(weights_in)
    for slot in range(2):
        projected = contract(qkv[slot], normed[...], 1, 0).astype(low)
        query_norm, query_inv = normalize_first(projected[:head].astype(wide))
        key_norm, key_inv = normalize_first(projected[head : 2 * head].astype(wide))
        values = projected[2 * head :]
        scores = contract(key_norm, query_norm, 0, 0, highest) * head ** (-0.5)
        exponent = jnp.exp(scores)
        attend = exponent / jnp.sum(exponent, 0, keepdims=True)
        attention[slot] = attend
        query[slot] = query_norm
        key[slot] = key_norm
        inverses[slot, 0:1, :] = query_inv
        inverses[slot, 1:2, :] = key_inv
        value[slot] = values
        heads[slot] = contract(values, attend.astype(low), 1, 0).astype(low)
    results_out += start_all(list(zip(kept[1:], results[1:])), sems, 8)
    both_heads = heads[...].reshape(2 * head, PATCHES)
    step = 768
    for n, start in enumerate(range(0, features, step)):
        both = out[:, :, start : start + step].reshape(2 * head, step)
        branch[start : start + step, :] = contract(both, both_heads, 0, 0).astype(low)
        part = pl.ds(start, step)
        results_out += start_all([(branch.at[part], branch_result.at[part])], sems, 14 + n)
    wait_all(results_out)


def backward_kernel(head, place, *refs):
    results, gathered, out_own, mine, theirs = refs[:7], refs[7], refs[8], refs[9], refs[10]
    shares, cotangent, out = refs[11:14]
    kept, sems = refs[14:21], refs[21]
    normed, attention, query, key, inverses, value, heads = kept
    core = place[0]
    thirds, quarter = 3 * head // 2, head // 2
    first_in = [(gathered.at[:, 1], cotangent), (out_own, out.at[0])]
    for source, at in partner_pieces(mine, theirs, core, thirds, quarter):
        first_in.append((source, out.at[1, at]))
    first_in = start_all(first_in, sems)
    kept_in = start_all(list(zip(results[1:], kept[1:])) + [(results[0], normed)], sems, 4)
    wait_all(first_in)
    scaling = head ** (-0.5)
    cores, _, chips, rows, columns = shares.shape
    cotangent = cotangent[...].reshape(normed.shape)
    grads = [contract(out[slot], cotangent, 1, 0).astype(low) for slot in range(2)]
    wait_all(kept_in[:-1])
    rights = []
    for slot, grad in enumerate(grads):
        attend = attention[slot]
        query_norm, key_norm = query[slot], key[slot]
        grad_weights = contract(value[slot], grad, 0, 0)
        grad_values = contract(grad, attend.astype(low), 1, 1)
        grad_scores = attend * (grad_weights - jnp.sum(grad_weights * attend, 0, keepdims=True))
        grad_qnorm = contract(key_norm, grad_scores, 1, 0, highest) * scaling
        grad_knorm = contract(query_norm, grad_scores, 1, 1, highest) * scaling
        grad_query = (
            grad_qnorm
            - jnp.mean(grad_qnorm, 0, keepdims=True)
            - query_norm * jnp.mean(grad_qnorm * query_norm, 0, keepdims=True)
        ) * inverses[slot, 0:1, :]
        grad_key = (
            grad_knorm
            - jnp.mean(grad_knorm, 0, keepdims=True)
            - key_norm * jnp.mean(grad_knorm * key_norm, 0, keepdims=True)
        ) * inverses[slot, 1:2, :]
        grad_proj = jnp.concatenate([grad_query, grad_key, grad_values], 0).astype(low)
        tail = jnp.concatenate([grad_proj[256:], jnp.zeros((columns - 3 * head, PATCHES), low)], 0)
        lead = jnp.concatenate([jnp.zeros((3 * head - 256, PATCHES), low), heads[slot]], 0)
        rights.append((grad_proj[:256], tail, lead))
    wait_all(kept_in[-1:])
    for slot, (main_right, tail, lead) in enumerate(rights):
        there = place[1 + slot]
        for owner in range(cores):
            for chip in range(chips):
                at = slice((2 * chip + owner) * rows, (2 * chip + owner + 1) * rows)
                main = normed[at, :]
                shares[owner, there, chip, :, :256] = contract(main, main_right, 1, 1).astype(low)
                shares[owner, there, chip, :, 256:] = (
                    contract(main, tail, 1, 1) + contract(cotangent[at, :], lead, 1, 1)
                ).astype(low)


def on_device(activations, w_qkv, w_out, d_branch):
    part, tokens = activations.shape
    features, head = w_out.shape
    images = tokens // PATCHES
    zh, xl, xh, y, core = (lax.axis_size(a) for a in ("zh", "xl", "xh", "y", "core"))
    swap = [(0, 1), (1, 0)]
    core_at, xl_at = lax.axis_index("core"), lax.axis_index("xl")
    place = jnp.stack([core_at, xl_at, 1 - xl_at]).astype(jnp.int32)

    cut = [slice(n * PATCHES, (n + 1) * PATCHES) for n in range(images)]
    both = jnp.concatenate([v[:, c] for c in cut for v in (activations, d_branch)], 0)
    mixed = lax.all_to_all(both.reshape(images, 2 * part, PATCHES), "xl", 0, 0, tiled=True)
    gathered = lax.all_gather(mixed.reshape(xl * 2 * part, PATCHES), Z, axis=0, tiled=True)
    gathered = gathered.reshape(features // part, 2, part, PATCHES)

    qkv_own, out_own = w_qkv.T, w_out.T
    thirds, quarter = 3 * head // 2, head // 2
    mine = jnp.concatenate(
        [
            lax.dynamic_slice_in_dim(qkv_own, core_at * thirds, thirds, 0),
            lax.dynamic_slice_in_dim(out_own, core_at * quarter, quarter, 0),
        ],
        0,
    )
    mine, mixed = lax.optimization_barrier((mine, mixed))
    mine = lax.ppermute(mine, "xl", swap)
    theirs = lax.ppermute(mine, "core", swap)

    shape = jax.ShapeDtypeStruct
    vmem = pl.BlockSpec(memory_space=pltpu.VMEM)
    smem = pl.BlockSpec(memory_space=pltpu.SMEM)
    hbm = pl.BlockSpec(memory_space=pltpu.HBM)
    kept = (
        shape((features, PATCHES), low),
        shape((2, PATCHES, PATCHES), wide),
        shape((2, head, PATCHES), wide),
        shape((2, head, PATCHES), wide),
        shape((2, 8, PATCHES), wide),
        shape((2, head, PATCHES), low),
        shape((2, head, PATCHES), low),
    )
    outputs = pl.pallas_call(
        functools.partial(forward_kernel, head),
        out_shape=kept + (shape((features, PATCHES), low),),
        in_specs=[smem] + [hbm] * 5,
        out_specs=[hbm] * 8,
        scratch_shapes=[
            pltpu.VMEM((features // part, part, PATCHES), low),
            pltpu.VMEM((2, 3 * head, features), low),
            pltpu.VMEM((2, head, features), low),
            pltpu.VMEM((features, PATCHES), low),
        ]
        + [pltpu.VMEM(k.shape, k.dtype) for k in kept]
        + [pltpu.SemaphoreType.DMA((18,))],
        compiler_params=pltpu.CompilerParams(vmem_limit_bytes=60 << 20),
        cost_estimate=pl.CostEstimate(
            flops=2_000_000_000, bytes_accessed=14_000_000, transcendentals=131072
        ),
        name="forward",
    )(place, gathered, qkv_own, out_own, mine, theirs)
    kept, branch = outputs[:7], outputs[7]
    summed = lax.psum_scatter(branch, Z, scatter_dimension=0, tiled=True)
    columns = 4 * head
    rows = features // (core * xh * y)
    shares = pl.pallas_call(
        functools.partial(backward_kernel, head),
        out_shape=shape((core, xl, xh * y, rows, columns), low),
        in_specs=[smem] + [hbm] * 11,
        out_specs=vmem,
        scratch_shapes=[
            pltpu.VMEM((features // part, part, PATCHES), low),
            pltpu.VMEM((2, head, features), low),
        ]
        + [pltpu.VMEM(k.shape, k.dtype) for k in kept]
        + [pltpu.SemaphoreType.DMA((11,))],
        compiler_params=pltpu.CompilerParams(vmem_limit_bytes=60 << 20),
        cost_estimate=pl.CostEstimate(
            flops=1_000_000, bytes_accessed=100_000, transcendentals=0
        ),
        name="backward",
    )(place, *kept, gathered, out_own, mine, theirs)
    pairs = lax.all_to_all(shares, "core", 0, 0, tiled=True)
    pair_sum = jnp.sum(pairs.astype(wide), 0).astype(low)
    grads = lax.all_to_all(
        pair_sum.reshape(xl * xh * y, rows, columns), ("xl", "xh", "y"), 0, 0, tiled=True
    )
    summed, grads = lax.optimization_barrier((summed, grads))
    grads = jnp.sum(grads.astype(wide), 0).astype(low)
    swapped = lax.all_to_all(summed.reshape(xl, part, PATCHES), "xl", 0, 0, tiled=True)
    branch_out = swapped.transpose(1, 0, 2).reshape(part, tokens)
    return (branch_out, grads[:, : 3 * head], grads[:, 3 * head :])


def solution(mesh):
    fine = Mesh(mesh.devices.reshape(2, 4, 2, 4, 4, 2), ("xh", "y", "core", "zh", "zl", "xl"))
    dp, mp = ("xh", "y", "core"), ("zh", "zl", "xl")
    in_specs = (P(mp, dp), P(None, mp), P(None, mp), P(mp, dp))
    out_specs = (P(mp, dp), P(dp, mp), P(dp, mp))
    return jax.shard_map(
        on_device, mesh=fine, in_specs=in_specs, out_specs=out_specs, check_vma=False
    )
```

```python
import functools

import jax
import jax.numpy as jnp
from jax import lax
from jax.experimental import pallas as pl
from jax.experimental.pallas import tpu as pltpu
from jax.sharding import Mesh
from jax.sharding import PartitionSpec as P

PATCHES = 256
GROUP = 4
epsilon = 1e-06
highest = lax.Precision.HIGHEST
low = jnp.bfloat16
wide = jnp.float32
Z = ("zh", "zl")


def contract(left, right, left_dim, right_dim, precision=None):
    return lax.dot_general(
        left,
        right,
        (((left_dim,), (right_dim,)), ((), ())),
        precision=precision,
        preferred_element_type=wide,
    )


def normalize_first(values):
    centre = values - jnp.mean(values, 0, keepdims=True)
    inverse = lax.rsqrt(jnp.mean(centre * centre, 0, keepdims=True) + epsilon)
    return (centre * inverse, inverse)


def aligned(start, size):
    return pl.ds(pl.multiple_of(start, 16), size)


SETS = ((0, 0, 4), (1, 0, 4), (2, 0, 4), (3, 0, 2), (3, 2, 2))


def start_all(pairs, sems, first=0):
    copies = [
        pltpu.make_async_copy(source, target, sems.at[first + n])
        for n, (source, target) in enumerate(pairs)
    ]
    for copy in copies:
        copy.start()
    return copies


def wait_all(copies):
    for copy in copies:
        copy.wait()


def partner_pieces(mine, theirs, core, first, size):
    for source, at in ((mine, core), (theirs, 1 - core)):
        yield source.at[pl.ds(first, size)], aligned(at * size, size)


def forward_kernel(head, place, *refs):
    sets, (qkv_own, out_own, mine, theirs) = refs[:5], refs[5:9]
    results, branch_result = refs[9:16], refs[16]
    raw, qkv, out, branch = refs[17:21]
    kept, sems = refs[21:28], refs[28]
    normed, attention, query, key, inverses, value, heads = kept
    features = normed.shape[0]
    block = features // (4 * GROUP)
    core = place[4]
    thirds, quarter = 3 * head // 2, head // 2
    rows_in = []
    for ref, (which, first, count) in zip(sets, SETS):
        for n in range(count):
            at = aligned((GROUP * (first + n) + place[which]) * block, block)
            rows_in.append((ref.at[pl.ds(block * n, block)], raw.at[at]))
    rows_in = start_all(rows_in, sems)
    weights_in = [(qkv_own, qkv.at[0]), (out_own, out.at[0])]
    for source, at in partner_pieces(mine, theirs, core, 0, thirds):
        weights_in.append((source, qkv.at[1, at]))
    for source, at in partner_pieces(mine, theirs, core, thirds, quarter):
        weights_in.append((source, out.at[1, at]))
    weights_in = start_all(weights_in, sems, 16)
    wait_all(rows_in)

    def rows_of(n):
        return raw[block * n : block * (n + 1), :].astype(wide)

    def fold(rows):
        return jnp.sum(rows.reshape(block // 8, 8, PATCHES), 0)

    blocks = range(4 * GROUP)
    mean = jnp.sum(sum(fold(rows_of(n)) for n in blocks), 0, keepdims=True) / features
    variance = sum(fold((rows_of(n) - mean) * (rows_of(n) - mean)) for n in blocks)
    scale = lax.rsqrt(jnp.sum(variance, 0, keepdims=True) / features + epsilon)
    for n in blocks:
        normed[block * n : block * (n + 1), :] = ((rows_of(n) - mean) * scale).astype(low)
    results_out = start_all([(normed, results[0])], sems, 22)
    wait_all(weights_in)
    for slot in range(2):
        projected = contract(qkv[slot], normed[...], 1, 0).astype(low)
        query_norm, query_inv = normalize_first(projected[:head].astype(wide))
        key_norm, key_inv = normalize_first(projected[head : 2 * head].astype(wide))
        values = projected[2 * head :]
        scores = contract(key_norm, query_norm, 0, 0, highest) * head ** (-0.5)
        exponent = jnp.exp(scores)
        attend = exponent / jnp.sum(exponent, 0, keepdims=True)
        attention[slot] = attend
        query[slot] = query_norm
        key[slot] = key_norm
        inverses[slot, 0:1, :] = query_inv
        inverses[slot, 1:2, :] = key_inv
        value[slot] = values
        heads[slot] = contract(values, attend.astype(low), 1, 0).astype(low)
    results_out += start_all(list(zip(kept[1:], results[1:])), sems, 23)
    both_heads = heads[...].reshape(2 * head, PATCHES)
    step = 768
    for n, start in enumerate(range(0, features, step)):
        both = out[:, :, start : start + step].reshape(2 * head, step)
        branch[start : start + step, :] = contract(both, both_heads, 0, 0).astype(low)
        part = pl.ds(start, step)
        results_out += start_all([(branch.at[part], branch_result.at[part])], sems, 29 + n)
    wait_all(results_out)


def backward_kernel(head, place, *refs):
    results, cotangent_in, out_own, mine, theirs = refs[:7], refs[7], refs[8], refs[9], refs[10]
    shares, cotangent, out = refs[11:14]
    kept, sems = refs[14:21], refs[21]
    normed, attention, query, key, inverses, value, heads = kept
    core = place[4]
    thirds, quarter = 3 * head // 2, head // 2
    first_in = [(cotangent_in, cotangent), (out_own, out.at[0])]
    for source, at in partner_pieces(mine, theirs, core, thirds, quarter):
        first_in.append((source, out.at[1, at]))
    first_in = start_all(first_in, sems)
    kept_in = start_all(list(zip(results[1:], kept[1:])) + [(results[0], normed)], sems, 4)
    wait_all(first_in)
    scaling = head ** (-0.5)
    cores, _, chips, rows, columns = shares.shape
    grads = [contract(out[slot], cotangent[...], 1, 0).astype(low) for slot in range(2)]
    wait_all(kept_in[:-1])
    rights = []
    for slot, grad in enumerate(grads):
        attend = attention[slot]
        query_norm, key_norm = query[slot], key[slot]
        grad_weights = contract(value[slot], grad, 0, 0)
        grad_values = contract(grad, attend.astype(low), 1, 1)
        grad_scores = attend * (grad_weights - jnp.sum(grad_weights * attend, 0, keepdims=True))
        grad_qnorm = contract(key_norm, grad_scores, 1, 0, highest) * scaling
        grad_knorm = contract(query_norm, grad_scores, 1, 1, highest) * scaling
        grad_query = (
            grad_qnorm
            - jnp.mean(grad_qnorm, 0, keepdims=True)
            - query_norm * jnp.mean(grad_qnorm * query_norm, 0, keepdims=True)
        ) * inverses[slot, 0:1, :]
        grad_key = (
            grad_knorm
            - jnp.mean(grad_knorm, 0, keepdims=True)
            - key_norm * jnp.mean(grad_knorm * key_norm, 0, keepdims=True)
        ) * inverses[slot, 1:2, :]
        grad_proj = jnp.concatenate([grad_query, grad_key, grad_values], 0).astype(low)
        tail = jnp.concatenate([grad_proj[256:], jnp.zeros((columns - 3 * head, PATCHES), low)], 0)
        lead = jnp.concatenate([jnp.zeros((3 * head - 256, PATCHES), low), heads[slot]], 0)
        rights.append((grad_proj[:256], tail, lead))
    wait_all(kept_in[-1:])
    for slot, (main_right, tail, lead) in enumerate(rights):
        there = place[5 + slot]
        for owner in range(cores):
            for chip in range(chips):
                at = slice((2 * chip + owner) * rows, (2 * chip + owner + 1) * rows)
                main = normed[at, :]
                shares[owner, there, chip, :, :256] = contract(main, main_right, 1, 1).astype(low)
                shares[owner, there, chip, :, 256:] = (
                    contract(main, tail, 1, 1) + contract(cotangent[at, :], lead, 1, 1)
                ).astype(low)


def shift(values, by):
    size = lax.axis_size(Z)
    return lax.ppermute(values, Z, [(i, (i + by) % size) for i in range(size)])


def on_device(activations, w_qkv, w_out, d_branch):
    part, tokens = activations.shape
    features, head = w_out.shape
    images = tokens // PATCHES
    zh, xl, xh, y, core = (lax.axis_size(a) for a in ("zh", "xl", "xh", "y", "core"))
    swap = [(0, 1), (1, 0)]
    core_at, xl_at, residue = (lax.axis_index(a) for a in ("core", "xl", "zl"))
    place = jnp.stack(
        [
            residue,
            (residue + 1) % GROUP,
            (residue + 3) % GROUP,
            (residue + 2) % GROUP,
            core_at,
            xl_at,
            1 - xl_at,
        ]
    ).astype(jnp.int32)

    cut = [slice(n * PATCHES, (n + 1) * PATCHES) for n in range(images)]
    both = jnp.concatenate([v[:, c] for c in cut for v in (activations, d_branch)], 0)
    both = both.reshape(images, 2, part, PATCHES)
    mixed = lax.all_to_all(both, "xl", 0, 0, tiled=True)

    qkv_own, out_own = w_qkv.T, w_out.T
    thirds, quarter = 3 * head // 2, head // 2
    mine = jnp.concatenate(
        [
            lax.dynamic_slice_in_dim(qkv_own, core_at * thirds, thirds, 0),
            lax.dynamic_slice_in_dim(out_own, core_at * quarter, quarter, 0),
        ],
        0,
    )
    mine, mixed = lax.optimization_barrier((mine, mixed))
    chunk = xl * part
    cotangent = lax.all_gather(mixed[:, 1].reshape(chunk, PATCHES), Z, axis=0, tiled=True)
    mine = lax.ppermute(mine, "xl", swap)
    same = lax.all_gather(mixed[:, 0].reshape(chunk, PATCHES), "zh", axis=0, tiled=True)
    mine, same = lax.optimization_barrier((mine, same))
    theirs = lax.ppermute(mine, "core", swap)
    middle = zh * chunk // 2
    sets = (
        same,
        shift(same, -1),
        shift(same, 1),
        shift(same[:middle], 2),
        shift(same[middle:], -2),
    )

    shape = jax.ShapeDtypeStruct
    vmem = pl.BlockSpec(memory_space=pltpu.VMEM)
    smem = pl.BlockSpec(memory_space=pltpu.SMEM)
    hbm = pl.BlockSpec(memory_space=pltpu.HBM)
    kept = (
        shape((features, PATCHES), low),
        shape((2, PATCHES, PATCHES), wide),
        shape((2, head, PATCHES), wide),
        shape((2, head, PATCHES), wide),
        shape((2, 8, PATCHES), wide),
        shape((2, head, PATCHES), low),
        shape((2, head, PATCHES), low),
    )
    outputs = pl.pallas_call(
        functools.partial(forward_kernel, head),
        out_shape=kept + (shape((features, PATCHES), low),),
        in_specs=[smem] + [hbm] * 9,
        out_specs=[hbm] * 8,
        scratch_shapes=[
            pltpu.VMEM((features, PATCHES), low),
            pltpu.VMEM((2, 3 * head, features), low),
            pltpu.VMEM((2, head, features), low),
            pltpu.VMEM((features, PATCHES), low),
        ]
        + [pltpu.VMEM(k.shape, k.dtype) for k in kept]
        + [pltpu.SemaphoreType.DMA((33,))],
        compiler_params=pltpu.CompilerParams(vmem_limit_bytes=60 << 20),
        cost_estimate=pl.CostEstimate(
            flops=2_000_000_000, bytes_accessed=14_000_000, transcendentals=131072
        ),
        name="forward",
    )(place, *sets, qkv_own, out_own, mine, theirs)
    kept, branch = outputs[:7], outputs[7]
    summed = lax.psum_scatter(branch, Z, scatter_dimension=0, tiled=True)
    columns = 4 * head
    rows = features // (core * xh * y)
    shares = pl.pallas_call(
        functools.partial(backward_kernel, head),
        out_shape=shape((core, xl, xh * y, rows, columns), low),
        in_specs=[smem] + [hbm] * 11,
        out_specs=vmem,
        scratch_shapes=[
            pltpu.VMEM((features, PATCHES), low),
            pltpu.VMEM((2, head, features), low),
        ]
        + [pltpu.VMEM(k.shape, k.dtype) for k in kept]
        + [pltpu.SemaphoreType.DMA((11,))],
        compiler_params=pltpu.CompilerParams(vmem_limit_bytes=60 << 20),
        cost_estimate=pl.CostEstimate(
            flops=1_000_000, bytes_accessed=100_000, transcendentals=0
        ),
        name="backward",
    )(place, *kept, cotangent, out_own, mine, theirs)
    pairs = lax.all_to_all(shares, "core", 0, 0, tiled=True)
    pair_sum = jnp.sum(pairs.astype(wide), 0).astype(low)
    grads = lax.all_to_all(
        pair_sum.reshape(xl * xh * y, rows, columns), ("xl", "xh", "y"), 0, 0, tiled=True
    )
    summed, grads = lax.optimization_barrier((summed, grads))
    grads = jnp.sum(grads.astype(wide), 0).astype(low)
    swapped = lax.all_to_all(summed.reshape(xl, part, PATCHES), "xl", 0, 0, tiled=True)
    branch_out = swapped.transpose(1, 0, 2).reshape(part, tokens)
    return (branch_out, grads[:, : 3 * head], grads[:, 3 * head :])


def solution(mesh):
    fine = Mesh(mesh.devices.reshape(2, 4, 2, 4, 4, 2), ("xh", "y", "core", "zh", "zl", "xl"))
    dp, mp = ("xh", "y", "core"), ("zh", "zl", "xl")
    in_specs = (P(mp, dp), P(None, mp), P(None, mp), P(mp, dp))
    out_specs = (P(mp, dp), P(dp, mp), P(dp, mp))
    return jax.shard_map(
        on_device, mesh=fine, in_specs=in_specs, out_specs=out_specs, check_vma=False
    )
```

```python
import functools

import jax
import jax.numpy as jnp
from jax import lax
from jax.experimental import pallas as pl
from jax.experimental.pallas import tpu as pltpu
from jax.sharding import Mesh
from jax.sharding import PartitionSpec as P

PATCHES = 256
GROUP = 4
epsilon = 1e-06
highest = lax.Precision.HIGHEST
low = jnp.bfloat16
wide = jnp.float32
Z = ("zh", "zl")


def contract(left, right, left_dim, right_dim, precision=None):
    return lax.dot_general(
        left,
        right,
        (((left_dim,), (right_dim,)), ((), ())),
        precision=precision,
        preferred_element_type=wide,
    )


def normalize_first(values):
    centre = values - jnp.mean(values, 0, keepdims=True)
    inverse = lax.rsqrt(jnp.mean(centre * centre, 0, keepdims=True) + epsilon)
    return (centre * inverse, inverse)


def aligned(start, size):
    return pl.ds(pl.multiple_of(start, 16), size)


SETS = ((0, 0, 4), (1, 0, 4), (2, 0, 4), (3, 0, 2), (3, 2, 2))


def start_all(pairs, sems, first=0):
    copies = [
        pltpu.make_async_copy(source, target, sems.at[first + n])
        for n, (source, target) in enumerate(pairs)
    ]
    for copy in copies:
        copy.start()
    return copies


def wait_all(copies):
    for copy in copies:
        copy.wait()


def partner_pieces(mine, theirs, core, first, size):
    for source, at in ((mine, core), (theirs, 1 - core)):
        yield source.at[pl.ds(first, size)], aligned(at * size, size)


def forward_kernel(head, place, *refs):
    sets, (qkv_own, out_own, mine, theirs) = refs[:5], refs[5:9]
    results, branch_result = refs[9:16], refs[16]
    raw, qkv, out, branch = refs[17:21]
    kept, sems = refs[21:28], refs[28]
    normed, attention, query, key, inverses, value, heads = kept
    features = normed.shape[0]
    block = features // (4 * GROUP)
    core = place[4]
    thirds, quarter = 3 * head // 2, head // 2
    half = block // 2
    rows_in = []
    for ref, (which, first, count) in zip(sets, SETS):
        for n in range(2 * count):
            at = (GROUP * (first + n // 2) + place[which]) * block + place[5 + n % 2] * half
            rows_in.append((ref.at[pl.ds(half * n, half)], raw.at[aligned(at, half)]))
    rows_in = start_all(rows_in, sems)
    weights_in = [(qkv_own, qkv.at[0])]
    for source, at in partner_pieces(mine, theirs, core, 0, thirds):
        weights_in.append((source, qkv.at[1, at]))
    weights_in.append((out_own, out.at[0]))
    for source, at in partner_pieces(mine, theirs, core, thirds, quarter):
        weights_in.append((source, out.at[1, at]))
    weights_in = start_all(weights_in, sems, 32)
    wait_all(rows_in)

    def rows_of(n):
        return raw[block * n : block * (n + 1), :].astype(wide)

    def fold(rows):
        return jnp.sum(rows.reshape(block // 8, 8, PATCHES), 0)

    blocks = range(4 * GROUP)
    mean = jnp.sum(sum(fold(rows_of(n)) for n in blocks), 0, keepdims=True) / features
    variance = sum(fold((rows_of(n) - mean) * (rows_of(n) - mean)) for n in blocks)
    scale = lax.rsqrt(jnp.sum(variance, 0, keepdims=True) / features + epsilon)
    for n in blocks:
        normed[block * n : block * (n + 1), :] = ((rows_of(n) - mean) * scale).astype(low)
    wait_all(weights_in[:3])
    both = contract(qkv[...].reshape(6 * head, features), normed[...], 1, 0).astype(low)
    for slot in range(2):
        projected = both[3 * head * slot : 3 * head * (slot + 1)]
        query_norm, query_inv = normalize_first(projected[:head].astype(wide))
        key_norm, key_inv = normalize_first(projected[head : 2 * head].astype(wide))
        values = projected[2 * head :]
        scores = contract(key_norm, query_norm, 0, 0, highest) * head ** (-0.5)
        exponent = jnp.exp(scores)
        attend = exponent / jnp.sum(exponent, 0, keepdims=True)
        attention[slot] = attend
        query[slot] = query_norm
        key[slot] = key_norm
        inverses[slot, 0:1, :] = query_inv
        inverses[slot, 1:2, :] = key_inv
        value[slot] = values
        heads[slot] = contract(values, attend.astype(low), 1, 0).astype(low)
    results_out = start_all(list(zip(kept[1:], results[1:])), sems, 39)
    results_out += start_all([(normed, results[0])], sems, 38)
    wait_all(weights_in[3:])
    both_heads = heads[...].reshape(2 * head, PATCHES)
    step = 768
    for n, start in enumerate(range(0, features, step)):
        both = out[:, :, start : start + step].reshape(2 * head, step)
        branch[start : start + step, :] = contract(both, both_heads, 0, 0).astype(low)
        part = pl.ds(start, step)
        results_out += start_all([(branch.at[part], branch_result.at[part])], sems, 45 + n)
    wait_all(results_out)


def backward_kernel(head, place, *refs):
    results, cotangent_in, out_own, mine, theirs = refs[:7], refs[7], refs[8], refs[9], refs[10]
    shares, cotangent, out = refs[11:14]
    kept, sems = refs[14:21], refs[21]
    normed, attention, query, key, inverses, value, heads = kept
    core = place[4]
    thirds, quarter = 3 * head // 2, head // 2
    first_in = [(cotangent_in.at[:, n], cotangent.at[:, place[5 + n]]) for n in range(2)]
    first_in.append((out_own, out.at[0]))
    for source, at in partner_pieces(mine, theirs, core, thirds, quarter):
        first_in.append((source, out.at[1, at]))
    first_in = start_all(first_in, sems)
    kept_in = start_all(list(zip(results[1:], kept[1:])) + [(results[0], normed)], sems, 5)
    wait_all(first_in)
    scaling = head ** (-0.5)
    cores, _, chips, rows, columns = shares.shape
    cotangent = cotangent[...].reshape(normed.shape)
    grads = [contract(out[slot], cotangent, 1, 0).astype(low) for slot in range(2)]
    wait_all(kept_in[:-1])
    rights = []
    for slot, grad in enumerate(grads):
        attend = attention[slot]
        query_norm, key_norm = query[slot], key[slot]
        grad_weights = contract(value[slot], grad, 0, 0)
        grad_values = contract(grad, attend.astype(low), 1, 1)
        grad_scores = attend * (grad_weights - jnp.sum(grad_weights * attend, 0, keepdims=True))
        grad_qnorm = contract(key_norm, grad_scores, 1, 0, highest) * scaling
        grad_knorm = contract(query_norm, grad_scores, 1, 1, highest) * scaling
        grad_query = (
            grad_qnorm
            - jnp.mean(grad_qnorm, 0, keepdims=True)
            - query_norm * jnp.mean(grad_qnorm * query_norm, 0, keepdims=True)
        ) * inverses[slot, 0:1, :]
        grad_key = (
            grad_knorm
            - jnp.mean(grad_knorm, 0, keepdims=True)
            - key_norm * jnp.mean(grad_knorm * key_norm, 0, keepdims=True)
        ) * inverses[slot, 1:2, :]
        grad_proj = jnp.concatenate([grad_query, grad_key, grad_values], 0).astype(low)
        tail = jnp.concatenate([grad_proj[256:], jnp.zeros((columns - 3 * head, PATCHES), low)], 0)
        lead = jnp.concatenate([jnp.zeros((3 * head - 256, PATCHES), low), heads[slot]], 0)
        rights.append((grad_proj[:256], tail, lead))
    wait_all(kept_in[-1:])
    for slot, (main_right, tail, lead) in enumerate(rights):
        there = place[5 + slot]
        for owner in range(cores):
            for chip in range(chips):
                at = slice((2 * chip + owner) * rows, (2 * chip + owner + 1) * rows)
                main = normed[at, :]
                shares[owner, there, chip, :, :256] = contract(main, main_right, 1, 1).astype(low)
                shares[owner, there, chip, :, 256:] = (
                    contract(main, tail, 1, 1) + contract(cotangent[at, :], lead, 1, 1)
                ).astype(low)


def shift(values, by):
    size = lax.axis_size(Z)
    return lax.ppermute(values, Z, [(i, (i + by) % size) for i in range(size)])


def on_device(activations, w_qkv, w_out, d_branch):
    part, tokens = activations.shape
    features, head = w_out.shape
    images = tokens // PATCHES
    zh, xl, xh, y, core = (lax.axis_size(a) for a in ("zh", "xl", "xh", "y", "core"))
    swap = [(0, 1), (1, 0)]
    core_at, xl_at, residue = (lax.axis_index(a) for a in ("core", "xl", "zl"))
    place = jnp.stack(
        [
            residue,
            (residue + 1) % GROUP,
            (residue + 3) % GROUP,
            (residue + 2) % GROUP,
            core_at,
            xl_at,
            1 - xl_at,
        ]
    ).astype(jnp.int32)

    def exchange(values):
        kept_image = lax.dynamic_slice_in_dim(values, xl_at * PATCHES, PATCHES, 1)
        other_image = lax.dynamic_slice_in_dim(values, (1 - xl_at) * PATCHES, PATCHES, 1)
        return jnp.concatenate([kept_image, lax.ppermute(other_image, "xl", swap)], 0)

    cot_block, act_block = exchange(d_branch), exchange(activations)

    qkv_own, out_own = w_qkv.T, w_out.T
    thirds, quarter = 3 * head // 2, head // 2
    mine = jnp.concatenate(
        [
            lax.dynamic_slice_in_dim(qkv_own, core_at * thirds, thirds, 0),
            lax.dynamic_slice_in_dim(out_own, core_at * quarter, quarter, 0),
        ],
        0,
    )
    mine, cot_block, act_block = lax.optimization_barrier((mine, cot_block, act_block))
    cotangent = lax.all_gather(cot_block, Z, axis=0, tiled=True)
    cotangent = cotangent.reshape(features // (xl * part), xl, part, PATCHES)
    mine = lax.ppermute(mine, "xl", swap)
    same = lax.all_gather(act_block, "zh", axis=0, tiled=True)
    mine, same = lax.optimization_barrier((mine, same))
    theirs = lax.ppermute(mine, "core", swap)
    middle = same.shape[0] // 2
    sets = (
        same,
        shift(same, -1),
        shift(same, 1),
        shift(same[:middle], 2),
        shift(same[middle:], -2),
    )

    shape = jax.ShapeDtypeStruct
    vmem = pl.BlockSpec(memory_space=pltpu.VMEM)
    smem = pl.BlockSpec(memory_space=pltpu.SMEM)
    hbm = pl.BlockSpec(memory_space=pltpu.HBM)
    kept = (
        shape((features, PATCHES), low),
        shape((2, PATCHES, PATCHES), wide),
        shape((2, head, PATCHES), wide),
        shape((2, head, PATCHES), wide),
        shape((2, 8, PATCHES), wide),
        shape((2, head, PATCHES), low),
        shape((2, head, PATCHES), low),
    )
    outputs = pl.pallas_call(
        functools.partial(forward_kernel, head),
        out_shape=kept + (shape((features, PATCHES), low),),
        in_specs=[smem] + [hbm] * 9,
        out_specs=[hbm] * 8,
        scratch_shapes=[
            pltpu.VMEM((features, PATCHES), low),
            pltpu.VMEM((2, 3 * head, features), low),
            pltpu.VMEM((2, head, features), low),
            pltpu.VMEM((features, PATCHES), low),
        ]
        + [pltpu.VMEM(k.shape, k.dtype) for k in kept]
        + [pltpu.SemaphoreType.DMA((49,))],
        compiler_params=pltpu.CompilerParams(vmem_limit_bytes=60 << 20),
        cost_estimate=pl.CostEstimate(
            flops=2_000_000_000, bytes_accessed=14_000_000, transcendentals=131072
        ),
        name="forward",
    )(place, *sets, qkv_own, out_own, mine, theirs)
    kept, branch = outputs[:7], outputs[7]
    summed = lax.psum_scatter(branch, Z, scatter_dimension=0, tiled=True)
    columns = 4 * head
    rows = features // (core * xh * y)
    shares = pl.pallas_call(
        functools.partial(backward_kernel, head),
        out_shape=shape((core, xl, xh * y, rows, columns), low),
        in_specs=[smem] + [hbm] * 11,
        out_specs=vmem,
        scratch_shapes=[
            pltpu.VMEM(cotangent.shape, low),
            pltpu.VMEM((2, head, features), low),
        ]
        + [pltpu.VMEM(k.shape, k.dtype) for k in kept]
        + [pltpu.SemaphoreType.DMA((12,))],
        compiler_params=pltpu.CompilerParams(vmem_limit_bytes=60 << 20),
        cost_estimate=pl.CostEstimate(
            flops=1_000_000, bytes_accessed=100_000, transcendentals=0
        ),
        name="backward",
    )(place, *kept, cotangent, out_own, mine, theirs)
    pairs = lax.all_to_all(shares, "core", 0, 0, tiled=True)
    pair_sum = jnp.sum(pairs.astype(wide), 0).astype(low)
    grads = lax.all_to_all(
        pair_sum.reshape(xl * xh * y, rows, columns), ("xl", "xh", "y"), 0, 0, tiled=True
    )
    summed, grads = lax.optimization_barrier((summed, grads))
    grads = jnp.sum(grads.astype(wide), 0).astype(low)
    swapped = lax.all_to_all(summed.reshape(xl, part, PATCHES), "xl", 0, 0, tiled=True)
    branch_out = swapped.transpose(1, 0, 2).reshape(part, tokens)
    return (branch_out, grads[:, : 3 * head], grads[:, 3 * head :])


def solution(mesh):
    fine = Mesh(mesh.devices.reshape(2, 4, 2, 4, 4, 2), ("xh", "y", "core", "zh", "zl", "xl"))
    dp, mp = ("xh", "y", "core"), ("zh", "zl", "xl")
    in_specs = (P(mp, dp), P(None, mp), P(None, mp), P(mp, dp))
    out_specs = (P(mp, dp), P(dp, mp), P(dp, mp))
    return jax.shard_map(
        on_device, mesh=fine, in_specs=in_specs, out_specs=out_specs, check_vma=False
    )
```

```python
import functools

import jax
import jax.numpy as jnp
from jax import lax
from jax.experimental import pallas as pl
from jax.experimental.pallas import tpu as pltpu
from jax.sharding import Mesh
from jax.sharding import PartitionSpec as P

PATCHES = 256
GROUP = 4
epsilon = 1e-06
highest = lax.Precision.HIGHEST
low = jnp.bfloat16
wide = jnp.float32
Z = ("zh", "zl")


def contract(left, right, left_dim, right_dim, precision=None):
    return lax.dot_general(
        left,
        right,
        (((left_dim,), (right_dim,)), ((), ())),
        precision=precision,
        preferred_element_type=wide,
    )


def normalize_first(values):
    centre = values - jnp.mean(values, 0, keepdims=True)
    inverse = lax.rsqrt(jnp.mean(centre * centre, 0, keepdims=True) + epsilon)
    return (centre * inverse, inverse)


def aligned(start, size):
    return pl.ds(pl.multiple_of(start, 16), size)


SETS = ((0, 0, 4), (1, 0, 4), (2, 0, 4), (3, 0, 2), (3, 2, 2))


def start_all(pairs, sems, first=0):
    copies = [
        pltpu.make_async_copy(source, target, sems.at[first + n])
        for n, (source, target) in enumerate(pairs)
    ]
    for copy in copies:
        copy.start()
    return copies


def wait_all(copies):
    for copy in copies:
        copy.wait()


def partner_pieces(mine, theirs, core, first, size):
    for source, at in ((mine, core), (theirs, 1 - core)):
        yield source.at[pl.ds(first, size)], aligned(at * size, size)


def forward_kernel(head, place, *refs):
    sets, (qkv_own, out_own, mine, theirs) = refs[:5], refs[5:9]
    results, branch_result = refs[9:16], refs[16]
    raw, qkv, out, branch = refs[17:21]
    kept, sems = refs[21:28], refs[28]
    normed, attention, query, key, inverses, value, heads = kept
    features = normed.shape[0]
    block = features // (4 * GROUP)
    core = place[4]
    thirds, quarter = 3 * head // 2, head // 2
    rows_in = []
    for ref, (which, first, count) in zip(sets, SETS):
        for n in range(count):
            at = aligned((GROUP * (first + n) + place[which]) * block, block)
            rows_in.append((ref.at[pl.ds(block * n, block)], raw.at[at]))
    rows_in = start_all(rows_in, sems)
    weights_in = [(qkv_own, qkv.at[0])]
    for source, at in partner_pieces(mine, theirs, core, 0, thirds):
        weights_in.append((source, qkv.at[1, at]))
    weights_in.append((out_own, out.at[0]))
    for source, at in partner_pieces(mine, theirs, core, thirds, quarter):
        weights_in.append((source, out.at[1, at]))
    weights_in = start_all(weights_in, sems, 16)
    wait_all(rows_in)

    def rows_of(n):
        return raw[block * n : block * (n + 1), :].astype(wide)

    def fold(rows):
        return jnp.sum(rows.reshape(block // 8, 8, PATCHES), 0)

    blocks = range(4 * GROUP)
    mean = jnp.sum(sum(fold(rows_of(n)) for n in blocks), 0, keepdims=True) / features
    variance = sum(fold((rows_of(n) - mean) * (rows_of(n) - mean)) for n in blocks)
    scale = lax.rsqrt(jnp.sum(variance, 0, keepdims=True) / features + epsilon)
    for n in blocks:
        normed[block * n : block * (n + 1), :] = ((rows_of(n) - mean) * scale).astype(low)
    wait_all(weights_in[:3])
    both = contract(qkv[...].reshape(6 * head, features), normed[...], 1, 0).astype(low)
    for slot in range(2):
        projected = both[3 * head * slot : 3 * head * (slot + 1)]
        query_norm, query_inv = normalize_first(projected[:head].astype(wide))
        key_norm, key_inv = normalize_first(projected[head : 2 * head].astype(wide))
        values = projected[2 * head :]
        scores = contract(key_norm, query_norm, 0, 0, highest) * head ** (-0.5)
        exponent = jnp.exp(scores)
        attend = exponent / jnp.sum(exponent, 0, keepdims=True)
        attention[slot] = attend
        query[slot] = query_norm
        key[slot] = key_norm
        inverses[slot, 0:1, :] = query_inv
        inverses[slot, 1:2, :] = key_inv
        value[slot] = values
        heads[slot] = contract(values, attend.astype(low), 1, 0).astype(low)
    results_out = start_all(list(zip(kept[1:], results[1:])), sems, 23)
    results_out += start_all([(normed, results[0])], sems, 22)
    wait_all(weights_in[3:])
    both_heads = heads[...].reshape(2 * head, PATCHES)
    step = 768
    for n, start in enumerate(range(0, features, step)):
        both = out[:, :, start : start + step].reshape(2 * head, step)
        branch[start : start + step, :] = contract(both, both_heads, 0, 0).astype(low)
        part = pl.ds(start, step)
        results_out += start_all([(branch.at[part], branch_result.at[part])], sems, 29 + n)
    wait_all(results_out)


def backward_kernel(head, place, *refs):
    results, cotangent_in, out_own, mine, theirs = refs[:7], refs[7], refs[8], refs[9], refs[10]
    shares, cotangent, out = refs[11:14]
    kept, sems = refs[14:21], refs[21]
    normed, attention, query, key, inverses, value, heads = kept
    core = place[4]
    thirds, quarter = 3 * head // 2, head // 2
    first_in = [(cotangent_in, cotangent), (out_own, out.at[0])]
    for source, at in partner_pieces(mine, theirs, core, thirds, quarter):
        first_in.append((source, out.at[1, at]))
    first_in = start_all(first_in, sems)
    kept_in = start_all(list(zip(results[1:], kept[1:])) + [(results[0], normed)], sems, 4)
    wait_all(first_in)
    scaling = head ** (-0.5)
    cores, _, chips, rows, columns = shares.shape
    grads = [contract(out[slot], cotangent[...], 1, 0).astype(low) for slot in range(2)]
    wait_all(kept_in[:-1])
    rights = []
    for slot, grad in enumerate(grads):
        attend = attention[slot]
        query_norm, key_norm = query[slot], key[slot]
        grad_weights = contract(value[slot], grad, 0, 0)
        grad_values = contract(grad, attend.astype(low), 1, 1)
        grad_scores = attend * (grad_weights - jnp.sum(grad_weights * attend, 0, keepdims=True))
        grad_qnorm = contract(key_norm, grad_scores, 1, 0, highest) * scaling
        grad_knorm = contract(query_norm, grad_scores, 1, 1, highest) * scaling
        grad_query = (
            grad_qnorm
            - jnp.mean(grad_qnorm, 0, keepdims=True)
            - query_norm * jnp.mean(grad_qnorm * query_norm, 0, keepdims=True)
        ) * inverses[slot, 0:1, :]
        grad_key = (
            grad_knorm
            - jnp.mean(grad_knorm, 0, keepdims=True)
            - key_norm * jnp.mean(grad_knorm * key_norm, 0, keepdims=True)
        ) * inverses[slot, 1:2, :]
        grad_proj = jnp.concatenate([grad_query, grad_key, grad_values], 0).astype(low)
        tail = jnp.concatenate([grad_proj[256:], jnp.zeros((columns - 3 * head, PATCHES), low)], 0)
        lead = jnp.concatenate([jnp.zeros((3 * head - 256, PATCHES), low), heads[slot]], 0)
        rights.append((grad_proj[:256], tail, lead))
    wait_all(kept_in[-1:])
    for slot, (main_right, tail, lead) in enumerate(rights):
        there = place[5 + slot]
        for owner in range(cores):
            for chip in range(chips):
                at = slice((2 * chip + owner) * rows, (2 * chip + owner + 1) * rows)
                main = normed[at, :]
                shares[owner, there, chip, :, :256] = contract(main, main_right, 1, 1).astype(low)
                shares[owner, there, chip, :, 256:] = (
                    contract(main, tail, 1, 1) + contract(cotangent[at, :], lead, 1, 1)
                ).astype(low)


def shift(values, by):
    size = lax.axis_size(Z)
    return lax.ppermute(values, Z, [(i, (i + by) % size) for i in range(size)])


def on_device(activations, w_qkv, w_out, d_branch):
    part, tokens = activations.shape
    features, head = w_out.shape
    images = tokens // PATCHES
    zh, xl, xh, y, core = (lax.axis_size(a) for a in ("zh", "xl", "xh", "y", "core"))
    swap = [(0, 1), (1, 0)]
    core_at, xl_at, residue = (lax.axis_index(a) for a in ("core", "xl", "zl"))
    place = jnp.stack(
        [
            residue,
            (residue + 1) % GROUP,
            (residue + 3) % GROUP,
            (residue + 2) % GROUP,
            core_at,
            xl_at,
            1 - xl_at,
        ]
    ).astype(jnp.int32)

    cut = [slice(n * PATCHES, (n + 1) * PATCHES) for n in range(images)]
    both = jnp.concatenate([v[:, c] for c in cut for v in (activations, d_branch)], 0)
    both = both.reshape(images, 2, part, PATCHES)
    mixed = lax.all_to_all(both, "xl", 0, 0, tiled=True)

    qkv_own, out_own = w_qkv.T, w_out.T
    thirds, quarter = 3 * head // 2, head // 2
    mine = jnp.concatenate(
        [
            lax.dynamic_slice_in_dim(qkv_own, core_at * thirds, thirds, 0),
            lax.dynamic_slice_in_dim(out_own, core_at * quarter, quarter, 0),
        ],
        0,
    )
    mine, mixed = lax.optimization_barrier((mine, mixed))
    chunk = xl * part
    cotangent = lax.all_gather(mixed[:, 1].reshape(chunk, PATCHES), Z, axis=0, tiled=True)
    mine = lax.ppermute(mine, "xl", swap)
    same = lax.all_gather(mixed[:, 0].reshape(chunk, PATCHES), "zh", axis=0, tiled=True)
    mine, same = lax.optimization_barrier((mine, same))
    theirs = lax.ppermute(mine, "core", swap)
    middle = zh * chunk // 2
    sets = (
        same,
        shift(same, -1),
        shift(same, 1),
        shift(same[:middle], 2),
        shift(same[middle:], -2),
    )

    shape = jax.ShapeDtypeStruct
    vmem = pl.BlockSpec(memory_space=pltpu.VMEM)
    smem = pl.BlockSpec(memory_space=pltpu.SMEM)
    hbm = pl.BlockSpec(memory_space=pltpu.HBM)
    kept = (
        shape((features, PATCHES), low),
        shape((2, PATCHES, PATCHES), wide),
        shape((2, head, PATCHES), wide),
        shape((2, head, PATCHES), wide),
        shape((2, 8, PATCHES), wide),
        shape((2, head, PATCHES), low),
        shape((2, head, PATCHES), low),
    )
    outputs = pl.pallas_call(
        functools.partial(forward_kernel, head),
        out_shape=kept + (shape((features, PATCHES), low),),
        in_specs=[smem] + [hbm] * 9,
        out_specs=[hbm] * 8,
        scratch_shapes=[
            pltpu.VMEM((features, PATCHES), low),
            pltpu.VMEM((2, 3 * head, features), low),
            pltpu.VMEM((2, head, features), low),
            pltpu.VMEM((features, PATCHES), low),
        ]
        + [pltpu.VMEM(k.shape, k.dtype) for k in kept]
        + [pltpu.SemaphoreType.DMA((33,))],
        compiler_params=pltpu.CompilerParams(vmem_limit_bytes=60 << 20),
        cost_estimate=pl.CostEstimate(
            flops=2_000_000_000, bytes_accessed=14_000_000, transcendentals=131072
        ),
        name="forward",
    )(place, *sets, qkv_own, out_own, mine, theirs)
    kept, branch = outputs[:7], outputs[7]
    summed = lax.psum_scatter(branch, Z, scatter_dimension=0, tiled=True)
    columns = 4 * head
    rows = features // (core * xh * y)
    shares = pl.pallas_call(
        functools.partial(backward_kernel, head),
        out_shape=shape((core, xl, xh * y, rows, columns), low),
        in_specs=[smem] + [hbm] * 11,
        out_specs=vmem,
        scratch_shapes=[
            pltpu.VMEM((features, PATCHES), low),
            pltpu.VMEM((2, head, features), low),
        ]
        + [pltpu.VMEM(k.shape, k.dtype) for k in kept]
        + [pltpu.SemaphoreType.DMA((11,))],
        compiler_params=pltpu.CompilerParams(vmem_limit_bytes=60 << 20),
        cost_estimate=pl.CostEstimate(
            flops=1_000_000, bytes_accessed=100_000, transcendentals=0
        ),
        name="backward",
    )(place, *kept, cotangent, out_own, mine, theirs)
    pairs = lax.all_to_all(shares, "core", 0, 0, tiled=True)
    pair_sum = jnp.sum(pairs.astype(wide), 0).astype(low)
    grads = lax.all_to_all(
        pair_sum.reshape(xl * xh * y, rows, columns), ("xl", "xh", "y"), 0, 0, tiled=True
    )
    summed, grads = lax.optimization_barrier((summed, grads))
    grads = jnp.sum(grads.astype(wide), 0).astype(low)
    swapped = lax.all_to_all(summed.reshape(xl, part, PATCHES), "xl", 0, 0, tiled=True)
    branch_out = swapped.transpose(1, 0, 2).reshape(part, tokens)
    return (branch_out, grads[:, : 3 * head], grads[:, 3 * head :])


def solution(mesh):
    fine = Mesh(mesh.devices.reshape(2, 4, 2, 4, 4, 2), ("xh", "y", "core", "zh", "zl", "xl"))
    dp, mp = ("xh", "y", "core"), ("zh", "zl", "xl")
    in_specs = (P(mp, dp), P(None, mp), P(None, mp), P(mp, dp))
    out_specs = (P(mp, dp), P(dp, mp), P(dp, mp))
    return jax.shard_map(
        on_device, mesh=fine, in_specs=in_specs, out_specs=out_specs, check_vma=False
    )
```
